32 devices in a mesh: ev: 2 (over y), mem: 16 (over z, x, core).
Axes of the slice: x: 2, y: 2, z: 4, core: 2. Of those that a mesh axis runs over, the one named last changes fastest.
Arguments:
- memory: bfloat16 [8192, 512], P(('ev', 'mem')), may hold values from -24 to 24
- last_time: int32 [8192], P(('ev', 'mem')), may hold values from 0 to 499
- event_time: int32 [4096], P(('ev', 'mem')), may hold values from 500 to 999
- edge_features: bfloat16 [4096, 48], P(('ev', 'mem')), may hold values from -6 to 6
- update_slot: int32 [4096, 2], P(('ev', 'mem')), may hold values from 0 to 511, as said below
- update_serve: int32 [32, 512], P(('ev', 'mem')), may hold values from -1 to 255, as said below
- lookup_slot: int32 [4096, 7], P(('ev', 'mem')), may hold values from 0 to 1791, as said below
- lookup_serve: int32 [32, 1792], P(('ev', 'mem')), may hold values from -1 to 255, as said below
- neighbour_gap: int32 [4096, 10], P(('ev', 'mem')), may hold values from 0 to 999
- hub_node: int32 [32], P(('ev', 'mem')), may hold values from 0 to 255
- hub_choice: int32 [4096, 4], P(('ev', 'mem')), may hold values from 0 to 31
- time_freq: float32 [100], replicated, may hold values from 0.001 to 0.3
- time_phase: float32 [100], replicated, may hold values from -3.140625 to 3.140625
- gru_weight: bfloat16 [1684, 1536], P(None, 'ev'), may hold values from -0.1875 to 0.1875
- gru_bias: float32 [2, 1536], replicated, may hold values from -3 to 3
- query_weight: bfloat16 [612, 256], replicated, may hold values from -0.25 to 0.25
- keyval_weight: bfloat16 [612, 512], replicated, may hold values from -0.25 to 0.25
- output_weight: bfloat16 [768, 512], replicated, may hold values from -0.21875 to 0.21875
Outputs:
- new_memory: bfloat16 [8192, 512], P(('ev', 'mem'))
- embedding: bfloat16 [4096, 512], P(('ev', 'mem'))
The draws below stay inside these ranges and needn't reach their ends.
Inputs may be any that keep to these rules, and one draw needn't show every extreme that they name: Within one device's events the values of update_slot are distinct; at most 16 of one device's endpoints go to one owner, and one owner, drawn from the seed, gets exactly 16 from every device. update_serve holds a local node exactly in the slots named by update_slot, -1 elsewhere; several slots may name the same node. Within one device's queries the values of lookup_slot are distinct; at most 56 of one device's lookups go to one owner, and one owner gets exactly 56 from every device. lookup_serve holds a local node exactly in the slots named by lookup_slot, -1 elsewhere.
All inputs are finite; a program needn't handle non-finite values.
Results may differ from the reference program's by a relative error of at most 0.011.
Values may be sent and summed in bfloat16 or wider, within the bound.
No kernel may reach another device: no remote copies, remote signals or barrier semaphores. Data moves between devices by JAX's collectives and lax.ppermute only.
A program may use at most 64 MiB of HBM per device.

```python
import math
import jax
import jax.numpy as jnp
from jax import lax

MEMW = 512
TW = 100
EF = 48
MSG = 1172
KEYW = 612
ATT = 256
HEADS = 2
HSIZE = 128
KN = 10
KHUB = 4
KROUTE = 7
EV_DEV = 128
NODE_DEV = 256
HUB_DEV = 1
HUBS = 32
EVENTS = 4096
NODES = 8192
CAP = 16
CAPN = 56
DEVICES = 32


def route_tables(key, capacity, columns):
    slot_total = DEVICES * capacity
    hot_owner = jax.random.randint(jax.random.fold_in(key, 7), (), 0, DEVICES)
    owners = jnp.arange(slot_total, dtype=jnp.int32) // capacity

    def for_device(device):
        dev_key = jax.random.fold_in(key, device + 100)
        ranking = jax.random.permutation(jax.random.fold_in(dev_key, 1), slot_total).astype(jnp.int32)
        ranking = jnp.where(owners == hot_owner, jnp.arange(slot_total, dtype=jnp.int32) % capacity - capacity, ranking)
        order = jnp.argsort(ranking, stable=True).astype(jnp.int32)
        chosen = order[:EV_DEV * columns]
        shuffle = jax.random.permutation(jax.random.fold_in(dev_key, 2), EV_DEV * columns)
        targets = chosen[shuffle]
        node_local = jax.random.randint(jax.random.fold_in(dev_key, 3), (slot_total,), 0, NODE_DEV)
        marked = jnp.zeros((slot_total,), jnp.int32).at[chosen].set(1)
        serving = jnp.where(marked > 0, node_local, -1).astype(jnp.int32)
        return (targets, serving)
    targets, serving = jax.vmap(for_device)(jnp.arange(DEVICES, dtype=jnp.int32))
    targets = targets.reshape(DEVICES * EV_DEV, columns).astype(jnp.int32)
    serving = serving.reshape(DEVICES, DEVICES, capacity).transpose(1, 0, 2).reshape(DEVICES, DEVICES * capacity)
    return (targets, serving)


def draw_update_slot(key, part):
    return route_tables(jax.random.fold_in(key, 11), CAP, 2)[0]


def draw_update_serve(key, part):
    return route_tables(jax.random.fold_in(key, 11), CAP, 2)[1]


def draw_lookup_slot(key, part):
    return route_tables(jax.random.fold_in(key, 13), CAPN, KROUTE)[0]


def draw_lookup_serve(key, part):
    return route_tables(jax.random.fold_in(key, 13), CAPN, KROUTE)[1]


def draw_memory(key, part):
    values = jnp.clip(jax.random.normal(jax.random.fold_in(key, 23), (NODES, MEMW), jnp.float32), -4.0, 4.0)
    return values.astype(jnp.bfloat16)


def touch_ends(array, own_key, smallest, top_value):
    longest = array.shape.index(max(array.shape))
    spots = []
    for shift in (0, 1):
        where = [jax.random.randint(jax.random.fold_in(own_key, axis), (), 0, length) for axis, length in enumerate(array.shape)]
        where[longest] = (where[longest] + shift) % array.shape[longest]
        spots.append(tuple(where))
    return array.at[spots[0]].set(smallest).at[spots[1]].set(top_value)


def shard_levels(rng, shape, pieces, least, top_value):
    gain = 1.0
    for dim, parts in pieces:
        steps = jax.random.uniform(jax.random.fold_in(jax.random.fold_in(rng, 6), dim), (parts,), jnp.float32, least / len(pieces), top_value / len(pieces))
        gain = gain * jnp.repeat(jnp.exp(steps), shape[dim] // parts).reshape((-1,) + (1,) * (len(shape) - 1 - dim))
    return gain


def scatter_about(stream_key, dims, spread, limit, pieces=(), kind=jnp.bfloat16):
    factor_of = shard_levels(stream_key, dims, pieces, -0.22, 0.18) if pieces else 1.0
    entries = jax.random.normal(stream_key, dims, jnp.float32) * spread * factor_of
    return jnp.minimum(jnp.maximum(entries, -limit), limit).astype(kind)


def setup_inputs(seed: int = 0) -> dict:
    key_of = jax.random.split(jax.random.key(seed), 19)
    memory = draw_memory(jax.random.fold_in(key_of[18], 71), 0)
    last_time = touch_ends(jax.random.randint(key_of[1], (NODES,), 0, 500), jax.random.fold_in(key_of[1], 1), 0, 499).astype(jnp.int32)
    event_time = touch_ends(jax.random.randint(key_of[2], (EVENTS,), 500, 1000), jax.random.fold_in(key_of[2], 1), 500, 999).astype(jnp.int32)
    edge_features = scatter_about(key_of[3], (EVENTS, EF), 1.0, 6.0, ((0, 32),))
    update_slot = draw_update_slot(jax.random.fold_in(key_of[18], 71), 0)
    update_serve = draw_update_serve(jax.random.fold_in(key_of[18], 71), 0)
    lookup_slot = draw_lookup_slot(jax.random.fold_in(key_of[18], 71), 0)
    lookup_serve = draw_lookup_serve(jax.random.fold_in(key_of[18], 71), 0)
    neighbour_gap = touch_ends(jax.random.randint(key_of[8], (EVENTS, KN), 0, 1000), jax.random.fold_in(key_of[8], 1), 0, 999).astype(jnp.int32)
    hub_node = touch_ends(jax.random.randint(key_of[9], (HUBS,), 0, NODE_DEV), jax.random.fold_in(key_of[9], 1), 0, NODE_DEV - 1).astype(jnp.int32)
    hub_choice = touch_ends(jax.random.randint(key_of[10], (EVENTS, KHUB), 0, HUBS), jax.random.fold_in(key_of[10], 1), 0, HUBS - 1).astype(jnp.int32)
    time_freq = jnp.clip(jnp.exp(jax.random.uniform(key_of[11], (TW,), jnp.float32, math.log(0.001), math.log(0.3))), 0.001, 0.3)
    time_phase = jnp.clip(jax.random.uniform(key_of[12], (TW,), jnp.float32, -3.140625, 3.140625), -3.140625, 3.140625)
    gru_weight = scatter_about(key_of[13], (MSG + MEMW, 3 * MEMW), MSG ** -0.5, 0.1875, ((1, 2),))
    gru_bias = scatter_about(key_of[14], (2, 3 * MEMW), 0.5, 3.0, (), jnp.float32)
    query_weight = scatter_about(key_of[15], (KEYW, ATT), KEYW ** -0.5, 0.25)
    keyval_weight = scatter_about(key_of[16], (KEYW, 2 * ATT), KEYW ** -0.5, 0.25)
    output_weight = scatter_about(key_of[17], (ATT + MEMW, MEMW), (ATT + MEMW) ** -0.5, 0.21875)
    return {"memory": memory, "last_time": last_time, "event_time": event_time, "edge_features": edge_features, "update_slot": update_slot, "update_serve": update_serve, "lookup_slot": lookup_slot, "lookup_serve": lookup_serve, "neighbour_gap": neighbour_gap, "hub_node": hub_node, "hub_choice": hub_choice, "time_freq": time_freq, "time_phase": time_phase, "gru_weight": gru_weight, "gru_bias": gru_bias, "query_weight": query_weight, "keyval_weight": keyval_weight, "output_weight": output_weight}


def encode(gap, time_freq, time_phase):
    return jnp.cos(gap.astype(jnp.float32)[..., None] * time_freq + time_phase).astype(jnp.bfloat16)


def gru_update(pre_in, pre_hid, previous_mem, counts):
    mem_width = previous_mem.shape[1]
    reset_gate = jax.nn.sigmoid(pre_in[:, :mem_width] + pre_hid[:, :mem_width])
    update_gate = jax.nn.sigmoid(pre_in[:, mem_width:2 * mem_width] + pre_hid[:, mem_width:2 * mem_width])
    candidate = jnp.tanh(pre_in[:, 2 * mem_width:] + reset_gate * pre_hid[:, 2 * mem_width:])
    previous = previous_mem.astype(jnp.float32)
    fresh = (1.0 - update_gate) * candidate + update_gate * previous
    return jnp.where(counts[:, None] > 0, fresh, previous).astype(jnp.bfloat16)


def node_ids(slot_table, serve_table, capacity):
    rows = slot_table.shape[0]
    device = (jnp.arange(rows, dtype=jnp.int32) // EV_DEV)[:, None]
    owner = slot_table // capacity
    slot = slot_table % capacity
    local = serve_table[owner, device * capacity + slot]
    return (owner * NODE_DEV + local).astype(jnp.int32)


def reference(memory, last_time, event_time, edge_features, update_slot, update_serve, lookup_slot, lookup_serve, neighbour_gap, hub_node, hub_choice, time_freq, time_phase, gru_weight, gru_bias, query_weight, keyval_weight, output_weight):
    ids_update = node_ids(update_slot, update_serve, CAP)
    device_rows = jnp.broadcast_to((jnp.arange(EVENTS, dtype=jnp.int32) // EV_DEV)[:, None], (EVENTS, 2))
    inverse = jnp.full((DEVICES, DEVICES * CAP), -1, jnp.int32)
    inverse = inverse.at[device_rows, update_slot].set(jnp.arange(EVENTS * 2, dtype=jnp.int32).reshape(EVENTS, 2))

    def owner_block(owner):
        column = jnp.arange(DEVICES * CAP, dtype=jnp.int32)
        requester = column // CAP
        slot = column % CAP
        endpoint = jnp.maximum(inverse[requester, owner * CAP + slot], 0)
        event = endpoint // 2
        side = endpoint % 2
        own_node = ids_update[event, side]
        other_node = ids_update[event, 1 - side]
        encoded = encode(event_time[event] - last_time[own_node], time_freq, time_phase)
        message = jnp.concatenate([memory[own_node], memory[other_node], encoded, edge_features[event]], axis=1)
        local = update_serve[owner]
        matches = jnp.arange(NODE_DEV, dtype=jnp.int32)[:, None] == local[None, :]
        summed = jnp.dot(matches.astype(jnp.bfloat16), message, preferred_element_type=jnp.float32)
        counts = jnp.sum(matches.astype(jnp.float32), axis=1)
        averaged = (summed / jnp.maximum(counts, 1.0)[:, None]).astype(jnp.bfloat16)
        block_mem = lax.dynamic_slice_in_dim(memory, owner * NODE_DEV, NODE_DEV, 0)
        pre_in = jnp.dot(averaged, gru_weight[:MSG], preferred_element_type=jnp.float32) + gru_bias[0]
        pre_hid = jnp.dot(block_mem, gru_weight[MSG:], preferred_element_type=jnp.float32) + gru_bias[1]
        return gru_update(pre_in, pre_hid, block_mem, counts)

    new_memory = lax.map(owner_block, jnp.arange(DEVICES, dtype=jnp.int32)).reshape(NODES, MEMW)
    hub_ids = ((jnp.arange(HUBS, dtype=jnp.int32) // HUB_DEV) * NODE_DEV + hub_node).astype(jnp.int32)
    hub_table = new_memory[hub_ids]
    ids_lookup = node_ids(lookup_slot, lookup_serve, CAPN)

    def event_block(device):
        start = (device * EV_DEV).astype(jnp.int32)
        block_ids = lax.dynamic_slice_in_dim(ids_lookup, start, EV_DEV, 0)
        block_hubs = lax.dynamic_slice_in_dim(hub_choice, start, EV_DEV, 0)
        block_gap = lax.dynamic_slice_in_dim(neighbour_gap, start, EV_DEV, 0)
        looked = new_memory[block_ids]
        self_row = looked[:, 0]
        neighbours = jnp.concatenate([looked[:, 1:], hub_table[block_hubs]], axis=1)
        key_input = jnp.concatenate([neighbours, encode(block_gap, time_freq, time_phase)], axis=2).reshape(EV_DEV * KN, KEYW)
        keyval = jnp.dot(key_input, keyval_weight, preferred_element_type=jnp.float32).astype(jnp.bfloat16).reshape(EV_DEV, KN, 2 * ATT)
        self_enc = encode(jnp.zeros((EV_DEV,), jnp.int32), time_freq, time_phase)
        queries = jnp.dot(jnp.concatenate([self_row, self_enc], axis=1), query_weight, preferred_element_type=jnp.float32).astype(jnp.bfloat16)
        query_heads = queries.reshape(EV_DEV, HEADS, HSIZE).astype(jnp.float32)
        key_heads = keyval[:, :, :ATT].reshape(EV_DEV, KN, HEADS, HSIZE).astype(jnp.float32)
        value_heads = keyval[:, :, ATT:].reshape(EV_DEV, KN, HEADS, HSIZE).astype(jnp.float32)
        scores = jnp.einsum("ehd,ekhd->ehk", query_heads, key_heads) * (HSIZE ** -0.5)
        scores = scores - jnp.max(scores, axis=2, keepdims=True)
        expo = jnp.exp(scores)
        prob = (expo / jnp.sum(expo, axis=2, keepdims=True)).astype(jnp.bfloat16)
        mixed = jnp.einsum("ehk,ekhd->ehd", prob.astype(jnp.float32), value_heads).astype(jnp.bfloat16).reshape(EV_DEV, ATT)
        return jnp.dot(jnp.concatenate([mixed, self_row], axis=1), output_weight, preferred_element_type=jnp.float32).astype(jnp.bfloat16)

    embedding = lax.map(event_block, jnp.arange(DEVICES, dtype=jnp.int32)).reshape(EVENTS, MEMW)
    return new_memory, embedding
```

```python
import functools

import jax
import jax.numpy as jnp
from jax import lax
from jax.experimental import pallas as pl
from jax.experimental.pallas import tpu as pltpu
from jax.sharding import PartitionSpec as P

HEADS = 2
LANES = 128
BF = jnp.bfloat16
F32 = jnp.float32
BOTH = ("ev", "mem")
VMEM = pl.BlockSpec(memory_space=pltpu.VMEM)
SMEM = pl.BlockSpec(memory_space=pltpu.SMEM)
PARAMS = pltpu.CompilerParams(vmem_limit_bytes=48 * 1024 * 1024)


def dot(a, b):
    return jnp.dot(a, b, preferred_element_type=F32)


def columns(row):
    parts = []
    for start in range(0, row.shape[1], LANES):
        part = jnp.broadcast_to(row[:, start : start + LANES], (LANES, LANES))
        parts.append(part.T)
    return jnp.concatenate(parts, axis=0)


def one_hot(column, width):
    lane = lax.broadcasted_iota(jnp.int32, column.shape, 1).astype(F32)
    parts = [(column - start == lane).astype(F32).astype(BF) for start in range(0, width, LANES)]
    return jnp.concatenate(parts, axis=1)


def one_hot_rows(row, height):
    line = lax.broadcasted_iota(jnp.int32, (height, row.shape[1]), 0).astype(F32)
    return (line == row).astype(F32)


def serve_kernel(serve_ref, time_ref, memory_ref, rows_ref, tau_ref):
    picks = one_hot(columns(serve_ref[...]), memory_ref.shape[0])
    rows_ref[...] = dot(picks, memory_ref[...]).astype(BF)
    tau = jnp.sum(picks.astype(F32) * time_ref[...], axis=1, keepdims=True)
    tau_ref[...] = jnp.broadcast_to(tau, tau_ref.shape)


def partner_kernel(slot_ref, extra_ref, fetched_ref, out_ref):
    total = fetched_ref.shape[0]
    fetched = fetched_ref[...]
    ends = [
        dot(one_hot(columns(slot_ref[c : c + 1, :]), total), fetched).astype(BF) for c in range(2)
    ]
    spread = jnp.concatenate(
        [one_hot_rows(slot_ref[c : c + 1, :], total).astype(BF) for c in range(2)], axis=1
    )
    extra = extra_ref[...]
    table = jnp.concatenate(
        [
            jnp.concatenate([ends[1], extra], axis=1),
            jnp.concatenate([ends[0], extra], axis=1),
        ],
        axis=0,
    )
    out_ref[...] = dot(spread, table).astype(BF)


def update_kernel(
    enc_width,
    edge_width,
    place_ref,
    serve_ref,
    lookup_ref,
    freq_ref,
    phase_ref,
    bias_ref,
    tau_ref,
    message_ref,
    memory_ref,
    shifted_ref,
    *refs,
):
    weight_refs, (new_ref, served_ref, in_ref, hid_ref) = refs[:-4], refs[-4:]
    nodes, width = memory_ref.shape
    lane = lax.broadcasted_iota(jnp.int32, tau_ref.shape, 1)
    rest = enc_width + edge_width - LANES
    match = one_hot_rows(serve_ref[...], nodes)
    counts = jnp.sum(match, axis=1, keepdims=True)
    extra = message_ref[:, width:].astype(F32)
    stamp = extra[:, rest : rest + 1] * 8.0 + extra[:, rest + 1 : rest + 2]
    gap = stamp - tau_ref[...]
    enc = jnp.cos(gap * freq_ref[...] + phase_ref[...])
    mixed = jnp.where(lane < enc_width, enc, extra).astype(BF)
    tail = jnp.where(lane < rest, extra, 0.0).astype(BF)
    messages = jnp.concatenate([message_ref[:, :width], mixed, tail], axis=1)
    summed = dot(match.astype(BF), messages)
    averaged = (summed / jnp.maximum(counts, 1.0)).astype(BF)
    memory = memory_ref[...]
    msg_width = 2 * width + enc_width + edge_width
    base = 2 * width + LANES
    left = jnp.concatenate([memory, averaged], axis=1)[:, :msg_width]
    hid_left = shifted_ref[:, : rest + width]
    piece = in_ref.shape[2]
    number = 0
    for weight_ref in weight_refs:
        for start in range(0, weight_ref.shape[1], piece):
            cols = slice(start, start + piece)
            where = place_ref[number]
            in_ref[where] = dot(left, weight_ref[:msg_width, cols])
            hid_ref[where] = dot(hid_left, weight_ref[base : msg_width + width, cols])
            number += 1

    def third(ref, row, index):
        parts = []
        at, end = index * width, (index + 1) * width
        while at < end:
            inside = at % piece
            size = min(piece - inside, end - at)
            parts.append(ref[at // piece, :, inside : inside + size])
            at += size
        joined = parts[0] if len(parts) == 1 else jnp.concatenate(parts, axis=1)
        return joined + bias_ref[row : row + 1, index * width : end]

    reset = jax.nn.sigmoid(third(in_ref, 0, 0) + third(hid_ref, 1, 0))
    keep = jax.nn.sigmoid(third(in_ref, 0, 1) + third(hid_ref, 1, 1))
    fresh = jnp.tanh(third(in_ref, 0, 2) + reset * third(hid_ref, 1, 2))
    previous = memory.astype(F32)
    fresh = (1.0 - keep) * fresh + keep * previous
    new = jnp.where(counts > 0.0, fresh, previous).astype(BF)
    new_ref[...] = new
    served_ref[...] = dot(one_hot(columns(lookup_ref[...]), nodes), new).astype(BF)


def attend_kernel(
    index_ref,
    hub_ref,
    gap_ref,
    freq_ref,
    phase_ref,
    looked_ref,
    query_ref,
    keyval_ref,
    output_ref,
    out_ref,
):
    owners, block, width = looked_ref.shape
    routes, events = index_ref.shape
    hubs, near = hub_ref.shape[0], gap_ref.shape[0]
    att = query_ref.shape[1]
    head = att // HEADS
    key_width = query_ref.shape[0]
    hub_from = max(block - 16, 0)
    hub_block = block - hub_from
    looked = looked_ref[...].reshape(owners * block, width)
    hub_rows = looked_ref[:, hub_from:, :].reshape(owners * hub_block, width)
    picks = jnp.concatenate(
        [one_hot(columns(index_ref[k : k + 1, :]), owners * block) for k in range(routes)], axis=0
    )
    rows = dot(picks, looked).astype(BF)
    hub_picks = jnp.concatenate(
        [one_hot(columns(hub_ref[k : k + 1, :]), owners * hub_block) for k in range(hubs)], axis=0
    )
    hub_near = dot(hub_picks, hub_rows).astype(BF)
    freq, phase = freq_ref[...], phase_ref[...]
    enc = jnp.concatenate(
        [jnp.cos(columns(gap_ref[k : k + 1, :]) * freq + phase) for k in range(near)], axis=0
    ).astype(BF)
    own = rows[:events]
    near_rows = jnp.concatenate([rows[events:], hub_near], axis=0)
    key_input = jnp.concatenate([near_rows, enc], axis=1)[:, :key_width]
    keyval = dot(key_input, keyval_ref[...]).astype(BF).astype(F32)
    own_enc = jnp.broadcast_to(jnp.cos(phase), (events, LANES)).astype(BF)
    query_input = jnp.concatenate([own, own_enc], axis=1)[:, :key_width]
    query = dot(query_input, query_ref[...]).astype(BF).astype(F32)
    mixed = []
    for h in range(HEADS):
        cols = slice(h * head, (h + 1) * head)
        vals = slice(att + h * head, att + (h + 1) * head)
        slabs = [slice(k * events, (k + 1) * events) for k in range(near)]
        scores = [
            jnp.sum(query[:, cols] * keyval[s, cols], axis=1, keepdims=True) * head**-0.5
            for s in slabs
        ]
        top = functools.reduce(jnp.maximum, scores)
        expo = [jnp.exp(s - top) for s in scores]
        total = functools.reduce(jnp.add, expo)
        prob = [(e / total).astype(BF).astype(F32) for e in expo]
        mixed.append(sum(p * keyval[s, vals] for p, s in zip(prob, slabs)))
    joined = jnp.concatenate([m.astype(BF) for m in mixed] + [own], axis=1)
    out_ref[...] = dot(joined, output_ref[...]).astype(BF)


def exchange(x):
    return lax.all_to_all(x, BOTH, split_axis=0, concat_axis=0, tiled=True)


def lanes(row):
    return jnp.pad(row, (0, LANES - row.shape[0]))[None, :]


def weight_pieces(gru_weight, ev_size, mem_size):
    half = gru_weight.shape[1] // 2
    if ev_size != 2 or mem_size % 2 or half % LANES:
        whole = lax.all_gather(gru_weight, "ev", axis=1, tiled=True)
        return [whole], whole.shape[1], jnp.zeros((1,), jnp.int32)
    ev, core = lax.axis_index("ev"), lax.axis_index("mem") % 2
    mine = lax.dynamic_slice_in_dim(gru_weight, core * half, half, axis=1)
    first = lax.ppermute(mine, "ev", [(0, 1), (1, 0)])
    second = lax.ppermute(first, "mem", [(i, i ^ 1) for i in range(mem_size)])
    other = 2 * (1 - ev)
    place = jnp.stack([2 * ev, 2 * ev + 1, other + core, other + 1 - core]).astype(jnp.int32)
    return [gru_weight, first, second], half, place


def local(
    memory,
    last_time,
    event_time,
    edge_features,
    update_slot,
    update_serve,
    lookup_slot,
    lookup_serve,
    neighbour_gap,
    hub_node,
    hub_choice,
    time_freq,
    time_phase,
    gru_weight,
    gru_bias,
    query_weight,
    keyval_weight,
    output_weight,
):
    ev_size = lax.axis_size("ev")
    mem_size = lax.axis_size("mem")
    devices = ev_size * mem_size
    nodes, width = memory.shape
    events = event_time.shape[0]
    slots = update_serve.shape[1]
    cap = slots // devices
    lookups = lookup_serve.shape[1]
    cap_lookup = lookups // devices
    enc_width = time_freq.shape[0]
    edge_width = edge_features.shape[1]
    freq, phase = lanes(time_freq), lanes(time_phase)

    pieces, piece, place = weight_pieces(gru_weight, ev_size, mem_size)

    serve_row = update_serve.astype(F32)
    rows, tau = pl.pallas_call(
        serve_kernel,
        out_shape=(
            jax.ShapeDtypeStruct((slots, width), BF),
            jax.ShapeDtypeStruct((slots, LANES), F32),
        ),
        in_specs=[VMEM] * 3,
        out_specs=(VMEM, VMEM),
        compiler_params=PARAMS,
        name="serve_endpoints",
    )(serve_row, last_time.astype(F32)[None, :], memory)
    fetched = exchange(rows.reshape(devices, cap, width)).reshape(slots, width)

    first_edges = LANES - enc_width
    rest = edge_width - first_edges
    stamps = jnp.stack([event_time // 8, event_time % 8], axis=1).astype(BF)
    extra = jnp.concatenate(
        [
            edge_features[:, first_edges:],
            stamps,
            jnp.zeros((events, LANES - edge_width - 2), BF),
            edge_features[:, :first_edges],
        ],
        axis=1,
    )
    message = pl.pallas_call(
        partner_kernel,
        out_shape=jax.ShapeDtypeStruct((slots, width + LANES), BF),
        in_specs=[VMEM] * 3,
        out_specs=VMEM,
        compiler_params=PARAMS,
        name="partner_rows",
    )(update_slot.T.astype(F32), extra, fetched)
    message = exchange(message.reshape(devices, cap, width + LANES)).reshape(slots, width + LANES)

    block = -(-(cap_lookup + 1) // 8) * 8
    lookup_row = jnp.concatenate(
        [
            lookup_serve.reshape(devices, cap_lookup),
            jnp.broadcast_to(hub_node[None, :], (devices, 1)),
            jnp.full((devices, block - cap_lookup - 1), -1, jnp.int32),
        ],
        axis=1,
    ).reshape(1, devices * block)
    shifted = jnp.pad(memory, ((0, 0), (rest, LANES - rest)))
    new_memory, served = pl.pallas_call(
        functools.partial(update_kernel, enc_width, edge_width),
        out_shape=(
            jax.ShapeDtypeStruct((nodes, width), BF),
            jax.ShapeDtypeStruct((devices * block, width), BF),
        ),
        in_specs=[SMEM] + [VMEM] * (9 + len(pieces)),
        out_specs=(VMEM, VMEM),
        scratch_shapes=[
            pltpu.VMEM((3 * width // piece, nodes, piece), F32),
            pltpu.VMEM((3 * width // piece, nodes, piece), F32),
        ],
        compiler_params=PARAMS,
        name="update_memory",
    )(
        place,
        serve_row,
        lookup_row.astype(F32),
        freq,
        phase,
        gru_bias,
        tau,
        message,
        memory,
        shifted,
        *pieces,
    )
    looked = exchange(served.reshape(devices, block, width))

    owner = lookup_slot // cap_lookup
    index = (owner * block + lookup_slot % cap_lookup).T.astype(F32)
    hub_from = max(block - 16, 0)
    hub_index = (hub_choice * (block - hub_from) + cap_lookup - hub_from).T.astype(F32)
    embedding = pl.pallas_call(
        attend_kernel,
        out_shape=jax.ShapeDtypeStruct((events, width), BF),
        in_specs=[VMEM] * 9,
        out_specs=VMEM,
        compiler_params=PARAMS,
        name="attend",
    )(
        index,
        hub_index,
        neighbour_gap.T.astype(F32),
        freq,
        phase,
        looked,
        query_weight,
        keyval_weight,
        output_weight,
    )
    return (new_memory, embedding)


def solution(mesh):
    both = P(BOTH)
    rows = P(BOTH, None)
    return jax.shard_map(
        local,
        mesh=mesh,
        in_specs=(
            rows,
            both,
            both,
            rows,
            rows,
            rows,
            rows,
            rows,
            rows,
            both,
            rows,
            P(),
            P(),
            P(None, "ev"),
            P(),
            P(),
            P(),
            P(),
        ),
        out_specs=(rows, rows),
        check_vma=False,
    )
```

```python
import functools
import math

import jax
import jax.numpy as jnp
from jax import lax
from jax.experimental import pallas as pl
from jax.experimental.pallas import tpu as pltpu
from jax.sharding import PartitionSpec as P

HEADS = 2
LANES = 128
SPLIT = 896
BF = jnp.bfloat16
F32 = jnp.float32
BOTH = ("ev", "hi", "lo")
NEAR = ("ev", "lo")
VMEM = pl.BlockSpec(memory_space=pltpu.VMEM)
SMEM = pl.BlockSpec(memory_space=pltpu.SMEM)
HBM = pl.BlockSpec(memory_space=pltpu.HBM)
MIB = 1024 * 1024


def dot(a, b):
    return jnp.dot(a, b, preferred_element_type=F32)


def dot_t(a, b):
    return lax.dot_general(a, b, (((1,), (1,)), ((), ())), preferred_element_type=F32)


def cosine(x):
    turns = jnp.floor(x * (0.5 / math.pi) + 0.5)
    rest = (x - turns * 6.28125) - turns * (2.0 * math.pi - 6.28125)
    square = rest * rest
    value = jnp.full_like(square, 1.0 / math.factorial(16))
    for order in range(14, -2, -2):
        sign = 1.0 if order % 4 == 0 else -1.0
        value = value * square + sign / math.factorial(order)
    return value


def sigmoid(x):
    return 0.5 * jnp.tanh(0.5 * x) + 0.5


def floor_div(x, n):
    return jnp.floor((x + 0.5) * (1.0 / n))


def columns(row):
    parts = []
    for start in range(0, row.shape[1], LANES):
        part = jnp.broadcast_to(row[:, start : start + LANES], (LANES, LANES))
        parts.append(part.T)
    return jnp.concatenate(parts, axis=0)


def one_hot(column, width):
    lane = lax.broadcasted_iota(jnp.int32, column.shape, 1).astype(F32)
    parts = [(column - start == lane).astype(F32).astype(BF) for start in range(0, width, LANES)]
    return jnp.concatenate(parts, axis=1)


def one_hot_rows(row, height):
    line = lax.broadcasted_iota(jnp.int32, (height, row.shape[1]), 0).astype(F32)
    return (line == row).astype(F32)


def lanes(row):
    return jnp.concatenate([row, jnp.zeros((1, LANES - row.shape[1]), row.dtype)], axis=1)


def fetch(pairs, sems):
    copies = [pltpu.make_async_copy(a, b, sems.at[i]) for i, (a, b) in enumerate(pairs)]
    for copy in copies:
        copy.start()
    return copies


def serve_kernel(serve_hbm, memory_hbm, rows_ref, serve, memory, sems):
    copies = fetch([(serve_hbm, serve), (memory_hbm, memory)], sems)
    copies[0].wait()
    picks = one_hot(columns(serve[...].astype(F32)), memory.shape[0])
    copies[1].wait()
    rows_ref[...] = dot(picks, memory[...]).astype(BF)


def prepare_kernel(
    enc_width,
    group,
    scalar_ref,
    serve_hbm,
    time_hbm,
    stamp_hbm,
    edge_hbm,
    slot_hbm,
    gap_hbm,
    lookup_hbm,
    freq_hbm,
    phase_hbm,
    tau_ref,
    enc_ref,
    swap_ref,
    sent_ref,
    near_ref,
    serve,
    time,
    stamp,
    edge,
    slot,
    gaps,
    lookup,
    freq,
    phase,
    column,
    sems,
):
    copies = fetch(
        [
            (serve_hbm, serve),
            (time_hbm, time),
            (stamp_hbm, stamp),
            (edge_hbm, edge),
            (slot_hbm, slot),
            (gap_hbm, gaps),
            (lookup_hbm, lookup),
            (freq_hbm, freq),
            (phase_hbm, phase),
        ],
        sems,
    )
    for copy in copies:
        copy.wait()
    picks = one_hot(columns(serve[...].astype(F32)), time.shape[1]).astype(F32)
    tau = jnp.sum(picks * time[...].astype(F32), axis=1, keepdims=True)
    tau_ref[...] = jnp.broadcast_to(tau, tau_ref.shape)
    events = gaps.shape[1]
    freq_row, phase_row = lanes(freq[...]), lanes(phase[...])
    for k in range(gaps.shape[0]):
        angle = columns(gaps[k : k + 1, :].astype(F32)) * freq_row + phase_row
        enc_ref[k * events : (k + 1) * events, :] = cosine(angle).astype(BF)
    first, second = (
        one_hot_rows(slot[c : c + 1, :].astype(F32), swap_ref.shape[0]) for c in range(2)
    )
    ends = jnp.concatenate([first, second], axis=1).astype(BF)
    others = jnp.concatenate([second, first], axis=1).astype(BF)
    swap_ref[...] = dot_t(ends, others).astype(BF)
    edges = edge.shape[0]
    first_edges = LANES - enc_width
    rest = edges - first_edges
    line = lax.broadcasted_iota(jnp.int32, (LANES, edges), 0)
    entry = lax.broadcasted_iota(jnp.int32, (LANES, edges), 1)
    wanted = jnp.where(line >= enc_width, line - enc_width, line + first_edges)
    shown = (line >= enc_width) | (line < rest)
    spread = ((wanted == entry) & shown).astype(F32).astype(BF)
    extra = dot(spread, edge[...])
    stamps = stamp[...].astype(F32)
    high = floor_div(stamps, 8)
    line = lax.broadcasted_iota(jnp.int32, extra.shape, 0)
    extra = jnp.where(line == rest, high, extra)
    extra = jnp.where(line == rest + 1, stamps - 8.0 * high, extra)
    sent_ref[...] = dot_t((first + second).astype(BF), extra.astype(BF)).astype(BF)
    column[...] = columns(lookup[...].astype(F32))
    own_half(scalar_ref[0], column, near_ref, group)


def own_half(hi, column, near_ref, group):
    for e in range(near_ref.shape[0] // group):
        start = pl.multiple_of((2 * e + hi) * group, 8)
        near_ref[e * group : (e + 1) * group, :] = column[pl.ds(start, group), :]


def partner_kernel(swap_ref, sent_ref, fetched_ref, out_ref):
    width = fetched_ref.shape[1]
    out_ref[:, :width] = dot(swap_ref[...], fetched_ref[...]).astype(BF)
    out_ref[:, width:] = sent_ref[...]


def update_kernel(
    enc_width,
    edge_width,
    shared,
    scalar_ref,
    hub_ref,
    serve_hbm,
    freq_hbm,
    phase_hbm,
    bias_hbm,
    memory_hbm,
    own_weight_hbm,
    tau_ref,
    near_ref,
    message_ref,
    *refs,
):
    count = 4 if shared else 1
    weight_refs, refs = refs[:count], refs[count:]
    new_ref, extended_ref, rows_ref, serve, freq, phase, bias, memory_ref, own_weight, pre, hid, sems = refs
    copies = fetch(
        [
            (serve_hbm, serve),
            (freq_hbm, freq),
            (phase_hbm, phase),
            (bias_hbm, bias),
            (memory_hbm, memory_ref),
        ]
        + ([(own_weight_hbm, own_weight)] if shared else []),
        sems,
    )
    for copy in copies[:5]:
        copy.wait()
    nodes, width = memory_ref.shape
    lane = lax.broadcasted_iota(jnp.int32, tau_ref.shape, 1)
    rest = enc_width + edge_width - LANES
    match = one_hot_rows(serve[...].astype(F32), nodes)
    counts = jnp.sum(match, axis=1, keepdims=True)
    extra = message_ref[:, width:].astype(F32)
    stamp = extra[:, rest : rest + 1] * 8.0 + extra[:, rest + 1 : rest + 2]
    gap = stamp - tau_ref[...]
    enc = cosine(gap * lanes(freq[...]) + lanes(phase[...]))
    mixed = jnp.where(lane < enc_width, enc, extra).astype(BF)
    tail = jnp.where(lane < rest, extra, 0.0).astype(BF)
    messages = jnp.concatenate([message_ref[:, :width], mixed, tail], axis=1)
    summed = dot(match.astype(BF), messages)
    averaged = (summed / jnp.maximum(counts, 1.0)).astype(BF)
    memory = memory_ref[...]
    msg_width = 2 * width + enc_width + edge_width
    left = jnp.concatenate([memory, averaged], axis=1)[:, :msg_width]
    hid_left = jnp.concatenate([jnp.zeros((nodes, rest), BF), memory], axis=1)
    piece = pre.shape[2]
    if shared:
        copies[5].wait()
        arrays = [(own_weight, own_weight, 0)]
        arrays += [(weight_refs[i], weight_refs[i + 1], SPLIT) for i in (0, 2)]
    else:
        arrays = [(weight_refs[0], weight_refs[0], 0)]
    number = 1
    for upper_ref, lower_ref, at in arrays:
        base = 2 * width + LANES - at
        for start in range(0, upper_ref.shape[1], piece):
            cols = slice(start, start + piece)
            where = scalar_ref[number]
            pre[where] = dot(left[:, :SPLIT], upper_ref[:SPLIT, cols]) + dot(
                left[:, SPLIT:], lower_ref[SPLIT - at : msg_width - at, cols]
            )
            hid[where] = dot(hid_left, lower_ref[base : base + rest + width, cols])
            number += 1

    def third(ref, row, index):
        parts = []
        at, end = index * width, (index + 1) * width
        while at < end:
            inside = at % piece
            size = min(piece - inside, end - at)
            parts.append(ref[at // piece, :, inside : inside + size])
            at += size
        joined = parts[0] if len(parts) == 1 else jnp.concatenate(parts, axis=1)
        return joined + bias[row : row + 1, index * width : end]

    reset = sigmoid(third(pre, 0, 0) + third(hid, 1, 0))
    keep = sigmoid(third(pre, 0, 1) + third(hid, 1, 1))
    fresh = jnp.tanh(third(pre, 0, 2) + reset * third(hid, 1, 2))
    previous = memory.astype(F32)
    fresh = (1.0 - keep) * fresh + keep * previous
    new = jnp.where(counts > 0.0, fresh, previous).astype(BF)
    new_ref[...] = new
    extended_ref[:nodes, :] = new
    line = lax.broadcasted_iota(jnp.int32, (16, nodes), 0)
    entry = lax.broadcasted_iota(jnp.int32, (16, nodes), 1)
    hub = ((entry == hub_ref[0]) & (line == 0)).astype(F32).astype(BF)
    extended_ref[nodes:, :] = dot(hub, new).astype(BF)
    rows_ref[...] = dot(one_hot(near_ref[...], nodes), new).astype(BF)


def far_kernel(group, scalar_ref, lookup_hbm, own_hbm, other_ref, out_ref, lookup, hub, column, far, sems):
    nodes = other_ref.shape[0] - 16
    copies = fetch([(lookup_hbm, lookup), (own_hbm.at[nodes:, :], hub)], sems)
    for copy in copies:
        copy.wait()
    column[...] = columns(lookup[...].astype(F32))
    own_half(scalar_ref[0], column, far, group)
    rows = dot(one_hot(far[...], nodes), other_ref[:nodes, :])
    near, block, width = out_ref.shape
    out_ref[:, : block - 8, :] = rows.reshape(near, block - 8, width).astype(BF)
    hubs = jnp.concatenate(
        [other_ref[nodes : nodes + 1, :], hub[0:1, :], jnp.zeros((6, width), BF)], axis=0
    )
    out_ref[:, block - 8 :, :] = jnp.broadcast_to(hubs[None], (near, 8, width))


def places(slot, hi, cap, lo_size):
    owner = floor_div(slot, cap)
    group = floor_div(owner, lo_size)
    ev = floor_div(group, 2)
    relay = ev * lo_size + owner - group * lo_size
    return relay, group - 2.0 * ev == hi, slot - cap * owner


def picks_of(index, width):
    return jnp.concatenate(
        [one_hot(columns(index[k : k + 1, :]), width) for k in range(index.shape[0])], axis=0
    )


def pick_kernel(cap, lo_size, scalar_ref, slot_ref, looked_ref, out_ref):
    owners, block, width = looked_ref.shape
    relay, near, place = places(slot_ref[...].astype(F32), scalar_ref[0].astype(F32), cap, lo_size)
    index = jnp.where(near, relay * block + place, -1.0)
    looked = looked_ref[...].reshape(owners * block, width)
    out_ref[...] = dot(picks_of(index, owners * block), looked).astype(BF)


def attend_kernel(
    cap,
    lo_size,
    scalar_ref,
    slot_hbm,
    hub_hbm,
    phase_hbm,
    query_hbm,
    keyval_hbm,
    output_hbm,
    enc_ref,
    picked_ref,
    looked_ref,
    out_ref,
    slot,
    hub,
    phase,
    query_ref,
    keyval_ref,
    output_ref,
    sems,
):
    copies = fetch(
        [
            (slot_hbm, slot),
            (hub_hbm, hub),
            (phase_hbm, phase),
            (keyval_hbm, keyval_ref),
            (query_hbm, query_ref),
            (output_hbm, output_ref),
        ],
        sems,
    )
    owners, block, width = looked_ref.shape
    routes, events = slot.shape
    near = routes - 1 + hub.shape[0]
    att = query_ref.shape[1]
    head = att // HEADS
    key_width = query_ref.shape[0]
    for copy in copies[:3]:
        copy.wait()
    hi = scalar_ref[0].astype(F32)
    relay, is_near, place = places(slot[...].astype(F32), hi, cap, lo_size)
    index = jnp.where(is_near, -1.0, relay * block + place)
    looked = looked_ref[...].reshape(owners * block, width)
    rows = (dot(picks_of(index, owners * block), looked) + picked_ref[...].astype(F32)).astype(BF)
    relay, is_near, place = places(hub[...].astype(F32), hi, 1, lo_size)
    hub_index = relay * 8.0 + jnp.where(is_near, 1.0, 0.0)
    hub_rows = looked_ref[:, block - 8 :, :].reshape(owners * 8, width)
    hub_near = dot(picks_of(hub_index, owners * 8), hub_rows).astype(BF)
    own = rows[:events]
    near_rows = jnp.concatenate([rows[events:], hub_near], axis=0)
    key_input = jnp.concatenate([near_rows, enc_ref[...]], axis=1)[:, :key_width]
    copies[3].wait()
    keyval = dot(key_input, keyval_ref[...]).astype(BF).astype(F32)
    own_enc = jnp.broadcast_to(cosine(lanes(phase[...])), (events, LANES)).astype(BF)
    query_input = jnp.concatenate([own, own_enc], axis=1)[:, :key_width]
    copies[4].wait()
    query = dot(query_input, query_ref[...]).astype(BF).astype(F32)
    mixed = []
    for h in range(HEADS):
        cols = slice(h * head, (h + 1) * head)
        vals = slice(att + h * head, att + (h + 1) * head)
        slabs = [slice(k * events, (k + 1) * events) for k in range(near)]
        scores = [
            jnp.sum(query[:, cols] * keyval[s, cols], axis=1, keepdims=True) * head**-0.5
            for s in slabs
        ]
        top = functools.reduce(jnp.maximum, scores)
        expo = [jnp.exp(s - top) for s in scores]
        total = functools.reduce(jnp.add, expo)
        prob = [(e / total).astype(BF).astype(F32) for e in expo]
        mixed.append(sum(p * keyval[s, vals] for p, s in zip(prob, slabs)))
    joined = jnp.concatenate([m.astype(BF) for m in mixed] + [own], axis=1)
    copies[5].wait()
    out_ref[...] = dot(joined, output_ref[...]).astype(BF)


def exchange(x, axes):
    return lax.all_to_all(x, axes, split_axis=0, concat_axis=0, tiled=True)


def after(x, *earlier):
    return lax.optimization_barrier((x, *earlier))[0]


def call(kernel, name, out_shape, smem, hbm, vmem, fetched=(), scratch=(), limit=20):
    many = isinstance(out_shape, tuple)
    copies = [pltpu.VMEM(x.shape, x.dtype) for x in fetched]
    sems = [pltpu.SemaphoreType.DMA((len(fetched),))] if fetched else []
    return pl.pallas_call(
        kernel,
        out_shape=out_shape,
        in_specs=[SMEM] * len(smem) + [HBM] * len(hbm) + [VMEM] * len(vmem),
        out_specs=(VMEM,) * len(out_shape) if many else VMEM,
        scratch_shapes=copies + list(scratch) + sems,
        compiler_params=pltpu.CompilerParams(vmem_limit_bytes=limit * MIB),
        name=name,
    )(*smem, *[pltpu.with_memory_space_constraint(x, pltpu.HBM) for x in hbm], *vmem)


def cores_share(gru_weight):
    half = gru_weight.shape[1] // 2
    return lax.axis_size("ev") == 2 and lax.axis_size("lo") % 2 == 0 and half % LANES == 0


def weight_rows(gru_weight, begin, end):
    half = gru_weight.shape[1] // 2
    core = lax.axis_index("lo") % 2
    mine = lax.dynamic_slice(gru_weight, (begin, core * half), (end - begin, half))
    return lax.ppermute(mine, "ev", [(0, 1), (1, 0)])


def other_core(x):
    return lax.ppermute(x, "lo", [(i, i ^ 1) for i in range(lax.axis_size("lo"))])


def other_half(x):
    return lax.ppermute(x, "hi", [(0, 1), (1, 0)])


def local(
    memory,
    last_time,
    event_time,
    edge_features,
    update_slot,
    update_serve,
    lookup_slot,
    lookup_serve,
    neighbour_gap,
    hub_node,
    hub_choice,
    time_freq,
    time_phase,
    gru_weight,
    gru_bias,
    query_weight,
    keyval_weight,
    output_weight,
):
    ev_size, hi_size, lo_size = (lax.axis_size(a) for a in BOTH)
    ev, hi, lo = (lax.axis_index(a) for a in BOTH)
    devices = ev_size * hi_size * lo_size
    near = ev_size * lo_size
    nodes, width = memory.shape
    events = event_time.shape[0]
    slots = update_serve.shape[1]
    cap = slots // devices
    cap_lookup = lookup_serve.shape[1] // devices
    block = -(-cap_lookup // 8) * 8
    group = lo_size * block
    enc_width = time_freq.shape[0]
    edge_width = edge_features.shape[1]
    freq, phase = time_freq[None, :], time_phase[None, :]
    shape, sent_shape = jax.ShapeDtypeStruct, pltpu.HBM

    rows = call(
        serve_kernel,
        "serve_endpoints",
        sent_shape((slots, width), BF),
        (),
        (update_serve, memory),
        (),
        fetched=(update_serve, memory),
    )
    shared = cores_share(gru_weight)
    if shared:
        late_weight = after(gru_weight, rows)
        upper = weight_rows(late_weight, 0, SPLIT)
        lower = weight_rows(late_weight, SPLIT, gru_weight.shape[0])
        piece = upper.shape[1]
        core, other = lo % 2, 2 * (1 - ev)
        place = [2 * ev, 2 * ev + 1, other + core, other + 1 - core]
    else:
        whole = lax.all_gather(gru_weight, "ev", axis=1, tiled=True)
        piece, place = whole.shape[1], [jnp.int32(0)]
    scalars = jnp.stack([hi] + place).astype(jnp.int32)
    fetched = exchange(rows.reshape(devices, cap, width), BOTH).reshape(slots, width)

    lookup_row = lookup_serve
    if block != cap_lookup:
        lookup_row = jnp.pad(
            lookup_serve.reshape(devices, cap_lookup),
            ((0, 0), (0, block - cap_lookup)),
            constant_values=-1,
        ).reshape(1, devices * block)
    late_lookup = after(lookup_row, rows)
    other_lookup = other_half(late_lookup)
    raw = (
        update_serve,
        last_time[None, :],
        event_time[None, :],
        edge_features.T,
        update_slot.T,
        neighbour_gap.T,
        late_lookup,
        freq,
        phase,
    )
    column = pltpu.VMEM((devices * block, LANES), F32)
    tau, enc, swap, sent, near_column = call(
        functools.partial(prepare_kernel, enc_width, group),
        "prepare",
        (
            shape((slots, LANES), F32),
            shape((events * neighbour_gap.shape[1], LANES), BF),
            shape((slots, slots), BF),
            shape((slots, LANES), BF),
            shape((near * block, LANES), F32),
        ),
        (scalars,),
        raw,
        (),
        fetched=raw,
        scratch=(column,),
    )
    message = call(
        partner_kernel,
        "partner_rows",
        sent_shape((slots, width + LANES), BF),
        (),
        (),
        (swap, sent, fetched),
    )
    if shared:
        upper, lower = after(upper, message), after(lower, message)
        pieces = [upper, lower, other_core(upper), other_core(lower)]
    else:
        pieces = [whole]
    message = exchange(message.reshape(devices, cap, width + LANES), BOTH)
    raw = (update_serve, freq, phase, gru_bias, memory, gru_weight)
    parts = pltpu.VMEM((3 * width // piece, nodes, piece), F32)
    new_memory, extended, near_rows = call(
        functools.partial(update_kernel, enc_width, edge_width, shared),
        "update_memory",
        (
            sent_shape((nodes, width), BF),
            sent_shape((nodes + 16, width), BF),
            sent_shape((near * block, width), BF),
        ),
        (scalars, hub_node),
        raw,
        (tau, near_column, message.reshape(slots, width + LANES), *pieces),
        fetched=raw,
        scratch=(parts, parts),
        limit=28,
    )
    other_extended = other_half(extended)
    near_looked = exchange(near_rows.reshape(near, block, width), NEAR)
    far_rows = call(
        functools.partial(far_kernel, group),
        "far_rows",
        sent_shape((near, block + 8, width), BF),
        (scalars,),
        (other_lookup, extended),
        (other_extended,),
        fetched=(other_lookup, shape((16, width), BF)),
        scratch=(column, pltpu.VMEM((near * block, LANES), F32)),
    )
    far_looked = exchange(far_rows, NEAR)
    slot_row = lookup_slot.T
    picked = call(
        functools.partial(pick_kernel, cap_lookup, lo_size),
        "pick_near",
        shape((lookup_slot.shape[1] * events, width), BF),
        (scalars,),
        (),
        (slot_row, near_looked),
    )
    raw = (slot_row, hub_choice.T, phase, query_weight, keyval_weight, output_weight)
    embedding = call(
        functools.partial(attend_kernel, cap_lookup, lo_size),
        "attend",
        sent_shape((events, width), BF),
        (scalars,),
        raw,
        (enc, picked, far_looked),
        fetched=raw,
    )
    return (new_memory, embedding)


def solution(mesh):
    ev_size, mem_size = mesh.devices.shape
    split = jax.sharding.Mesh(mesh.devices.reshape(ev_size, 2, mem_size // 2), BOTH)
    both = P(BOTH)
    rows = P(BOTH, None)
    return jax.shard_map(
        local,
        mesh=split,
        in_specs=(
            rows,
            both,
            both,
            rows,
            rows,
            rows,
            rows,
            rows,
            rows,
            both,
            rows,
            P(),
            P(),
            P(None, "ev"),
            P(),
            P(),
            P(),
            P(),
        ),
        out_specs=(rows, rows),
        check_vma=False,
    )
```

```python
import functools
import math

import jax
import jax.numpy as jnp
from jax import lax
from jax.experimental import pallas as pl
from jax.experimental.pallas import tpu as pltpu
from jax.sharding import PartitionSpec as P

HEADS = 2
LANES = 128
SHARED = 384
DIRECT = 2 * SHARED
BF = jnp.bfloat16
F32 = jnp.float32
BOTH = ("ev", "hi", "lo")
NEAR = ("ev", "lo")
VMEM = pl.BlockSpec(memory_space=pltpu.VMEM)
SMEM = pl.BlockSpec(memory_space=pltpu.SMEM)
HBM = pl.BlockSpec(memory_space=pltpu.HBM)
MIB = 1024 * 1024


def dot(a, b):
    return jnp.dot(a, b, preferred_element_type=F32)


def dot_t(a, b):
    return lax.dot_general(a, b, (((1,), (1,)), ((), ())), preferred_element_type=F32)


def cosine(x):
    turns = jnp.floor(x * (0.5 / math.pi) + 0.5)
    rest = (x - turns * 6.28125) - turns * (2.0 * math.pi - 6.28125)
    square = rest * rest
    value = jnp.full_like(square, 1.0 / math.factorial(16))
    for order in range(14, -2, -2):
        sign = 1.0 if order % 4 == 0 else -1.0
        value = value * square + sign / math.factorial(order)
    return value


def sigmoid(x):
    return 0.5 * jnp.tanh(0.5 * x) + 0.5


def floor_div(x, n):
    return jnp.floor((x + 0.5) * (1.0 / n))


def columns(row):
    parts = []
    for start in range(0, row.shape[1], LANES):
        part = jnp.broadcast_to(row[:, start : start + LANES], (LANES, LANES))
        parts.append(part.T)
    return jnp.concatenate(parts, axis=0)


def one_hot(column, width):
    lane = lax.broadcasted_iota(jnp.int32, column.shape, 1).astype(F32)
    parts = [(column - start == lane).astype(F32).astype(BF) for start in range(0, width, LANES)]
    return jnp.concatenate(parts, axis=1)


def one_hot_rows(row, height):
    line = lax.broadcasted_iota(jnp.int32, (height, row.shape[1]), 0).astype(F32)
    return (line == row).astype(F32)


def lanes(row):
    return jnp.concatenate([row, jnp.zeros((1, LANES - row.shape[1]), row.dtype)], axis=1)


def fetch(pairs, sems):
    copies = [pltpu.make_async_copy(a, b, sems.at[i]) for i, (a, b) in enumerate(pairs)]
    for copy in copies:
        copy.start()
    return copies


def serve_kernel(serve_hbm, memory_hbm, rows_ref, serve, memory, sems):
    copies = fetch([(serve_hbm, serve), (memory_hbm, memory)], sems)
    copies[0].wait()
    picks = one_hot(columns(serve[...].astype(F32)), memory.shape[0])
    copies[1].wait()
    rows_ref[...] = dot(picks, memory[...]).astype(BF)


def prepare_kernel(
    enc_width,
    group,
    scalar_ref,
    serve_hbm,
    time_hbm,
    stamp_hbm,
    edge_hbm,
    slot_hbm,
    lookup_hbm,
    freq_hbm,
    phase_hbm,
    tau_ref,
    swap_ref,
    sent_ref,
    near_hbm,
    serve,
    time,
    stamp,
    edge,
    slot,
    lookup,
    freq,
    phase,
    column,
    near,
    sems,
):
    copies = fetch(
        [
            (serve_hbm, serve),
            (time_hbm, time),
            (stamp_hbm, stamp),
            (edge_hbm, edge),
            (slot_hbm, slot),
            (lookup_hbm, lookup),
            (freq_hbm, freq),
            (phase_hbm, phase),
        ],
        sems,
    )
    for copy in copies:
        copy.wait()
    column[...] = columns(lookup[...].astype(F32))
    own_half(scalar_ref[0], column, near, group)
    out = pltpu.make_async_copy(near, near_hbm, sems.at[0])
    out.start()
    picks = one_hot(columns(serve[...].astype(F32)), time.shape[1]).astype(F32)
    tau = jnp.sum(picks * time[...].astype(F32), axis=1, keepdims=True)
    slots = serve.shape[1]
    tau_ref[:slots, :] = jnp.broadcast_to(tau, (slots, LANES))
    tau_ref[slots : slots + 8, :] = jnp.broadcast_to(lanes(freq[...]), (8, LANES))
    tau_ref[slots + 8 : slots + 16, :] = jnp.broadcast_to(lanes(phase[...]), (8, LANES))
    first, second = (
        one_hot_rows(slot[c : c + 1, :].astype(F32), swap_ref.shape[0]) for c in range(2)
    )
    ends = jnp.concatenate([first, second], axis=1).astype(BF)
    others = jnp.concatenate([second, first], axis=1).astype(BF)
    swap_ref[...] = dot_t(ends, others).astype(BF)
    edges = edge.shape[0]
    first_edges = LANES - enc_width
    rest = edges - first_edges
    line = lax.broadcasted_iota(jnp.int32, (LANES, edges), 0)
    entry = lax.broadcasted_iota(jnp.int32, (LANES, edges), 1)
    wanted = jnp.where(line >= enc_width, line - enc_width, line + first_edges)
    shown = (line >= enc_width) | (line < rest)
    spread = ((wanted == entry) & shown).astype(F32).astype(BF)
    extra = dot(spread, edge[...])
    stamps = stamp[...].astype(F32)
    high = floor_div(stamps, 8)
    line = lax.broadcasted_iota(jnp.int32, extra.shape, 0)
    extra = jnp.where(line == rest, high, extra)
    extra = jnp.where(line == rest + 1, stamps - 8.0 * high, extra)
    sent_ref[...] = dot_t((first + second).astype(BF), extra.astype(BF)).astype(BF)
    out.wait()


def own_half(hi, column, near_ref, group):
    for e in range(near_ref.shape[0] // group):
        start = pl.multiple_of((2 * e + hi) * group, 8)
        near_ref[e * group : (e + 1) * group, :] = column[pl.ds(start, group), :]


def partner_kernel(swap_ref, sent_ref, fetched_ref, out_ref):
    width = fetched_ref.shape[1]
    out_ref[:, :width] = dot(swap_ref[...], fetched_ref[...]).astype(BF)
    out_ref[:, width:] = sent_ref[...]


def update_kernel(
    enc_width,
    edge_width,
    shared,
    scalar_ref,
    hub_ref,
    serve_hbm,
    memory_hbm,
    bias_hbm,
    near_hbm,
    own_weight_hbm,
    tau_ref,
    message_ref,
    *refs,
):
    count = 6 if shared else 1
    weight_refs, refs = refs[:count], refs[count:]
    new_hbm, extended_hbm, rows_hbm, serve, memory_ref, bias, near_ref, own_weight = refs[:8]
    pre, hid, out, rows_out, sems = refs[8:]
    pairs = [(serve_hbm, serve), (memory_hbm, memory_ref), (bias_hbm, bias), (near_hbm, near_ref)]
    pairs += [(own_weight_hbm, own_weight)] if shared else []
    copies = fetch(pairs, sems)
    nodes, width = memory_ref.shape
    slots = message_ref.shape[0]
    lane = lax.broadcasted_iota(jnp.int32, (slots, LANES), 1)
    rest = enc_width + edge_width - LANES
    extra = message_ref[:, width:].astype(F32)
    stamp = extra[:, rest : rest + 1] * 8.0 + extra[:, rest + 1 : rest + 2]
    gap = stamp - tau_ref[:slots, :]
    enc = cosine(gap * tau_ref[slots : slots + 1, :] + tau_ref[slots + 8 : slots + 9, :])
    mixed = jnp.where(lane < enc_width, enc, extra).astype(BF)
    tail = jnp.where(lane < rest, extra, 0.0).astype(BF)
    messages = jnp.concatenate([message_ref[:, :width], mixed, tail], axis=1)
    copies[0].wait()
    match = one_hot_rows(serve[...].astype(F32), nodes)
    counts = jnp.sum(match, axis=1, keepdims=True)
    summed = dot(match.astype(BF), messages)
    averaged = (summed / jnp.maximum(counts, 1.0)).astype(BF)
    copies[1].wait()
    memory = memory_ref[...]
    msg_width = 2 * width + enc_width + edge_width
    base = 2 * width + LANES
    left = jnp.concatenate([memory, averaged], axis=1)[:, :msg_width]
    hid_left = jnp.concatenate([jnp.zeros((nodes, rest), BF), memory], axis=1)
    piece = pre.shape[2]

    def whole(number, weight_ref):
        for start in range(0, weight_ref.shape[1], piece):
            cols = slice(start, start + piece)
            where = scalar_ref[number]
            pre[where] = dot(left, weight_ref[:msg_width, cols])
            hid[where] = dot(hid_left, weight_ref[base : base + rest + width, cols])
            number += 1

    if shared:
        for number, (mine, other, lower) in ((3, weight_refs[:3]), (4, weight_refs[3:])):
            where = scalar_ref[number]
            side = scalar_ref[5]
            halves = [left[:, :SHARED], left[:, SHARED:DIRECT]]
            first = jnp.where(side == 0, halves[0], halves[1])
            second = jnp.where(side == 0, halves[1], halves[0])
            pre[where] = (
                dot(first, mine[...])
                + dot(second, other[...])
                + dot(left[:, DIRECT:], lower[: msg_width - DIRECT, :])
            )
            hid[where] = dot(hid_left, lower[base - DIRECT :, :])
        copies[4].wait()
        whole(1, own_weight)
    else:
        whole(1, weight_refs[0])
    copies[2].wait()

    def third(ref, row, index):
        parts = []
        at, end = index * width, (index + 1) * width
        while at < end:
            inside = at % piece
            size = min(piece - inside, end - at)
            parts.append(ref[at // piece, :, inside : inside + size])
            at += size
        joined = parts[0] if len(parts) == 1 else jnp.concatenate(parts, axis=1)
        return joined + bias[row : row + 1, index * width : end]

    reset = sigmoid(third(pre, 0, 0) + third(hid, 1, 0))
    keep = sigmoid(third(pre, 0, 1) + third(hid, 1, 1))
    fresh = jnp.tanh(third(pre, 0, 2) + reset * third(hid, 1, 2))
    previous = memory.astype(F32)
    fresh = (1.0 - keep) * fresh + keep * previous
    new = jnp.where(counts > 0.0, fresh, previous).astype(BF)
    out[:nodes, :] = new
    line = lax.broadcasted_iota(jnp.int32, (16, nodes), 0)
    entry = lax.broadcasted_iota(jnp.int32, (16, nodes), 1)
    hub = ((entry == hub_ref[0]) & (line == 0)).astype(F32).astype(BF)
    out[nodes:, :] = dot(hub, new).astype(BF)
    sends = [
        pltpu.make_async_copy(out, extended_hbm, sems.at[0]),
        pltpu.make_async_copy(out.at[:nodes, :], new_hbm, sems.at[1]),
    ]
    for send in sends:
        send.start()
    copies[3].wait()
    total = near_ref.shape[0]
    part = total // 2
    for i in range(2):
        some = slice(i * part, (i + 1) * part)
        rows_out[some, :] = dot(one_hot(near_ref[some, :], nodes), new).astype(BF)
        sends.append(pltpu.make_async_copy(rows_out.at[some, :], rows_hbm.at[some, :], sems.at[2 + i]))
        sends[-1].start()
    for send in sends:
        send.wait()


def far_kernel(group, scalar_ref, lookup_hbm, own_hbm, other_ref, out_ref, lookup, hub, column, far, sems):
    nodes = other_ref.shape[0] - 16
    copies = fetch([(lookup_hbm, lookup), (own_hbm.at[nodes:, :], hub)], sems)
    for copy in copies:
        copy.wait()
    column[...] = columns(lookup[...].astype(F32))
    own_half(scalar_ref[0], column, far, group)
    rows = dot(one_hot(far[...], nodes), other_ref[:nodes, :])
    near, block, width = out_ref.shape
    out_ref[:, : block - 8, :] = rows.reshape(near, block - 8, width).astype(BF)
    hubs = jnp.concatenate(
        [other_ref[nodes : nodes + 1, :], hub[0:1, :], jnp.zeros((6, width), BF)], axis=0
    )
    out_ref[:, block - 8 :, :] = jnp.broadcast_to(hubs[None], (near, 8, width))


def places(slot, hi, cap, lo_size):
    owner = floor_div(slot, cap)
    group = floor_div(owner, lo_size)
    ev = floor_div(group, 2)
    relay = ev * lo_size + owner - group * lo_size
    return relay, group - 2.0 * ev == hi, slot - cap * owner


def picks_of(index, width):
    return jnp.concatenate(
        [one_hot(columns(index[k : k + 1, :]), width) for k in range(index.shape[0])], axis=0
    )


def pick_kernel(
    cap,
    lo_size,
    scalar_ref,
    slot_hbm,
    hub_hbm,
    gap_hbm,
    freq_hbm,
    phase_hbm,
    looked_ref,
    picked_ref,
    far_ref,
    hub_ref,
    enc_ref,
    own_ref,
    slot,
    hub,
    gaps,
    freq,
    phase,
    sems,
):
    copies = fetch(
        [(slot_hbm, slot), (hub_hbm, hub), (gap_hbm, gaps), (freq_hbm, freq), (phase_hbm, phase)],
        sems,
    )
    for copy in copies:
        copy.wait()
    owners, block, width = looked_ref.shape
    hi = scalar_ref[0].astype(F32)
    relay, near, place = places(slot[...].astype(F32), hi, cap, lo_size)
    index = jnp.where(near, relay * block + place, -1.0)
    looked = looked_ref[...].reshape(owners * block, width)
    events = gaps.shape[1]
    picks = [one_hot(columns(index[k : k + 1, :]), owners * block) for k in range(slot.shape[0])]
    picked_ref[...] = dot(jnp.concatenate(picks, axis=0), looked).astype(BF)
    far_ref[...] = jnp.where(near, -1.0, relay * (block + 8) + place)
    relay, near, place = places(hub[...].astype(F32), hi, 1, lo_size)
    hub_ref[...] = relay * 8.0 + jnp.where(near, 1.0, 0.0)
    freq_row, phase_row = lanes(freq[...]), lanes(phase[...])
    for k in range(gaps.shape[0]):
        angle = columns(gaps[k : k + 1, :].astype(F32)) * freq_row + phase_row
        enc_ref[k * events : (k + 1) * events, :] = cosine(angle).astype(BF)
    own_ref[...] = jnp.broadcast_to(cosine(phase_row), (8, LANES)).astype(BF)


def attend_kernel(
    keyval_hbm,
    enc_hbm,
    query_hbm,
    output_hbm,
    picked_ref,
    far_ref,
    hub_ref,
    own_enc_ref,
    looked_ref,
    out_ref,
    keyval_ref,
    enc_ref,
    query_ref,
    output_ref,
    sems,
):
    copies = fetch(
        [
            (keyval_hbm, keyval_ref),
            (enc_hbm, enc_ref),
            (query_hbm, query_ref),
            (output_hbm, output_ref),
        ],
        sems,
    )
    owners, block, width = looked_ref.shape
    events = out_ref.shape[0]
    near = enc_ref.shape[0] // events
    att = query_ref.shape[1]
    head = att // HEADS
    looked = looked_ref[...].reshape(owners * block, width)
    hub_rows = looked_ref[:, block - 8 :, :].reshape(owners * 8, width)
    hub_near = dot(picks_of(hub_ref[...], owners * 8), hub_rows).astype(BF)
    picks = picks_of(far_ref[...], owners * block)
    rows = (dot(picks, looked) + picked_ref[...].astype(F32)).astype(BF)
    own = rows[:events]
    near_rows = jnp.concatenate([rows[events:], hub_near], axis=0)
    copies[0].wait()
    copies[1].wait()
    key_width = keyval_ref.shape[0]
    key_input = jnp.concatenate([near_rows, enc_ref[...]], axis=1)[:, :key_width]
    keyval = dot(key_input, keyval_ref[...]).astype(BF).astype(F32)
    copies[2].wait()
    own_enc = jnp.broadcast_to(own_enc_ref[0:1, :], (events, LANES))
    query_input = jnp.concatenate([own, own_enc], axis=1)[:, :key_width]
    query = dot(query_input, query_ref[...]).astype(BF).astype(F32)
    mixed = []
    for h in range(HEADS):
        cols = slice(h * head, (h + 1) * head)
        vals = slice(att + h * head, att + (h + 1) * head)
        slabs = [slice(k * events, (k + 1) * events) for k in range(near)]
        scores = [
            jnp.sum(query[:, cols] * keyval[s, cols], axis=1, keepdims=True) * head**-0.5
            for s in slabs
        ]
        top = functools.reduce(jnp.maximum, scores)
        expo = [jnp.exp(s - top) for s in scores]
        total = functools.reduce(jnp.add, expo)
        prob = [(e / total).astype(BF).astype(F32) for e in expo]
        mixed.append(sum(p * keyval[s, vals] for p, s in zip(prob, slabs)))
    joined = jnp.concatenate([m.astype(BF) for m in mixed] + [own], axis=1)
    copies[3].wait()
    out_ref[...] = dot(joined, output_ref[...]).astype(BF)


def exchange(x, axes):
    return lax.all_to_all(x, axes, split_axis=0, concat_axis=0, tiled=True)


def after(x, *earlier):
    return lax.optimization_barrier((x, *earlier))[0]


def call(kernel, name, out_shape, smem, hbm, vmem, fetched=(), scratch=(), left=(), kept=(), limit=20, extra_sems=0):
    many = isinstance(out_shape, tuple)
    specs = tuple(HBM if x in left else VMEM for x in range(len(out_shape))) if many else VMEM
    copies = [pltpu.VMEM(x.shape, x.dtype) for x in fetched]
    sems = [pltpu.SemaphoreType.DMA((len(fetched) + extra_sems,))] if fetched else []
    return pl.pallas_call(
        kernel,
        out_shape=out_shape,
        in_specs=[SMEM] * len(smem) + [HBM] * len(hbm) + [VMEM] * (len(kept) + len(vmem)),
        out_specs=specs,
        scratch_shapes=copies + list(scratch) + sems,
        compiler_params=pltpu.CompilerParams(vmem_limit_bytes=limit * MIB),
        name=name,
    )(*smem, *[pltpu.with_memory_space_constraint(x, pltpu.HBM) for x in hbm], *[pltpu.with_memory_space_constraint(x, pltpu.VMEM) for x in kept], *vmem)


def cores_share(gru_weight):
    half = gru_weight.shape[1] // 2
    return lax.axis_size("ev") == 2 and lax.axis_size("lo") % 4 == 0 and half % LANES == 0


def other_ev(x):
    return lax.ppermute(x, "ev", [(0, 1), (1, 0)])


def other_x(x):
    return lax.ppermute(x, "lo", [(i, i ^ 2) for i in range(lax.axis_size("lo"))])


def other_core(x):
    return lax.ppermute(x, "lo", [(i, i ^ 1) for i in range(lax.axis_size("lo"))])


def other_half(x):
    return lax.ppermute(x, "hi", [(0, 1), (1, 0)])


def local(
    memory,
    last_time,
    event_time,
    edge_features,
    update_slot,
    update_serve,
    lookup_slot,
    lookup_serve,
    neighbour_gap,
    hub_node,
    hub_choice,
    time_freq,
    time_phase,
    gru_weight,
    gru_bias,
    query_weight,
    keyval_weight,
    output_weight,
):
    ev_size, hi_size, lo_size = (lax.axis_size(a) for a in BOTH)
    ev, hi, lo = (lax.axis_index(a) for a in BOTH)
    devices = ev_size * hi_size * lo_size
    near = ev_size * lo_size
    nodes, width = memory.shape
    events = event_time.shape[0]
    slots = update_serve.shape[1]
    cap = slots // devices
    cap_lookup = lookup_serve.shape[1] // devices
    block = -(-cap_lookup // 8) * 8
    group = lo_size * block
    enc_width = time_freq.shape[0]
    edge_width = edge_features.shape[1]
    freq, phase = time_freq[None, :], time_phase[None, :]
    shape, sent_shape = jax.ShapeDtypeStruct, pltpu.HBM

    shared = cores_share(gru_weight)
    total, half = gru_weight.shape[0], gru_weight.shape[1] // 2
    rows = call(
        serve_kernel,
        "serve_endpoints",
        sent_shape((slots, width), BF),
        (),
        (update_serve, memory),
        (),
        fetched=(update_serve, memory),
    )
    if shared:
        late_weight = after(gru_weight, rows)
        side, column_at = lo // 2 % 2, lo % 2 * half
        first = other_ev(
            lax.dynamic_slice(late_weight, (side * SHARED, column_at), (SHARED, half))
        )
        piece = half
        core, other = lo % 2, 2 * (1 - ev)
        place = [2 * ev, 2 * ev + 1, other + core, other + 1 - core]
    else:
        whole = lax.all_gather(gru_weight, "ev", axis=1, tiled=True)
        piece, place = whole.shape[1], [jnp.int32(0)]
    scalars = jnp.stack([hi] + place + [lo // 2 % 2]).astype(jnp.int32)
    fetched = exchange(rows.reshape(devices, cap, width), BOTH).reshape(slots, width)

    lookup_row = lookup_serve
    if block != cap_lookup:
        lookup_row = jnp.pad(
            lookup_serve.reshape(devices, cap_lookup),
            ((0, 0), (0, block - cap_lookup)),
            constant_values=-1,
        ).reshape(1, devices * block)
    raw = (
        after(update_serve, rows),
        last_time[None, :],
        event_time[None, :],
        edge_features.T,
        update_slot.T,
        lookup_row,
        freq,
        phase,
    )
    tau, swap, sent, near_column = call(
        functools.partial(prepare_kernel, enc_width, group),
        "prepare",
        (
            pltpu.VMEM((slots + 16, LANES), F32),
            pltpu.VMEM((slots, slots), BF),
            pltpu.VMEM((slots, LANES), BF),
            sent_shape((near * block, LANES), F32),
        ),
        (scalars,),
        raw,
        (),
        fetched=raw,
        scratch=(
            pltpu.VMEM((devices * block, LANES), F32),
            pltpu.VMEM((near * block, LANES), F32),
        ),
        left=(3,),
    )
    if shared:
        sent = after(sent, first)
    message = call(
        partner_kernel,
        "partner_rows",
        sent_shape((slots, width + LANES), BF),
        (),
        (),
        (fetched,),
        kept=(swap, sent),
    )
    if shared:
        late_weight = after(gru_weight, rows)
        lower = other_ev(lax.dynamic_slice(late_weight, (DIRECT, column_at), (total - DIRECT, half)))
        first = after(first, message)
        second = other_x(first)
        pieces = [first, second, after(lower, second)]
        pieces += [other_core(x) for x in pieces]
    else:
        pieces = [whole]
    message = exchange(message.reshape(devices, cap, width + LANES), BOTH)
    raw = (update_serve, memory, gru_bias, near_column, gru_weight)
    parts = pltpu.VMEM((3 * width // piece, nodes, piece), F32)
    new_memory, extended, near_rows = call(
        functools.partial(update_kernel, enc_width, edge_width, shared),
        "update_memory",
        (
            sent_shape((nodes, width), BF),
            sent_shape((nodes + 16, width), BF),
            sent_shape((near * block, width), BF),
        ),
        (scalars, hub_node),
        raw,
        (message.reshape(slots, width + LANES), *pieces),
        kept=(tau,),
        fetched=raw,
        scratch=(
            parts,
            parts,
            pltpu.VMEM((nodes + 16, width), BF),
            pltpu.VMEM((near * block, width), BF),
        ),
        left=(0, 1, 2),
        limit=28,
    )
    other_extended = other_half(extended)
    near_looked = exchange(near_rows.reshape(near, block, width), NEAR)
    other_lookup = other_half(after(lookup_row, message))
    far_rows = call(
        functools.partial(far_kernel, group),
        "far_rows",
        sent_shape((near, block + 8, width), BF),
        (scalars,),
        (other_lookup, extended),
        (other_extended,),
        fetched=(other_lookup, shape((16, width), BF)),
        scratch=(
            pltpu.VMEM((devices * block, LANES), F32),
            pltpu.VMEM((near * block, LANES), F32),
        ),
    )
    far_looked = exchange(far_rows, NEAR)
    raw = (lookup_slot.T, hub_choice.T, neighbour_gap.T, freq, phase)
    routes, near_count = lookup_slot.shape[1] * events, neighbour_gap.shape[1] * events
    picked, far_index, hub_index, enc, own_enc = call(
        functools.partial(pick_kernel, cap_lookup, lo_size),
        "pick_near",
        (
            pltpu.VMEM((routes, width), BF),
            pltpu.VMEM(lookup_slot.T.shape, F32),
            pltpu.VMEM(hub_choice.T.shape, F32),
            sent_shape((near_count, LANES), BF),
            pltpu.VMEM((8, LANES), BF),
        ),
        (scalars,),
        raw,
        (near_looked,),
        fetched=raw,
    )
    raw = (keyval_weight, enc, query_weight, output_weight)
    embedding = call(
        attend_kernel,
        "attend",
        sent_shape((events, width), BF),
        (),
        raw,
        (far_looked,),
        kept=(picked, far_index, hub_index, own_enc),
        fetched=raw,
    )
    return (new_memory, embedding)


def solution(mesh):
    ev_size, mem_size = mesh.devices.shape
    split = jax.sharding.Mesh(mesh.devices.reshape(ev_size, 2, mem_size // 2), BOTH)
    both = P(BOTH)
    rows = P(BOTH, None)
    return jax.shard_map(
        local,
        mesh=split,
        in_specs=(
            rows,
            both,
            both,
            rows,
            rows,
            rows,
            rows,
            rows,
            rows,
            both,
            rows,
            P(),
            P(),
            P(None, "ev"),
            P(),
            P(),
            P(),
            P(),
        ),
        out_specs=(rows, rows),
        check_vma=False,
    )
```

```python
import functools
import math

import jax
import jax.numpy as jnp
from jax import lax
from jax.experimental import pallas as pl
from jax.experimental.pallas import tpu as pltpu
from jax.sharding import PartitionSpec as P

HEADS = 2
LANES = 128
SHARED = 384
DIRECT = 2 * SHARED
BF = jnp.bfloat16
F32 = jnp.float32
BOTH = ("ev", "hi", "low", "rest")
NEAR = ("ev", "rest", "low")
VMEM = pl.BlockSpec(memory_space=pltpu.VMEM)
SMEM = pl.BlockSpec(memory_space=pltpu.SMEM)
HBM = pl.BlockSpec(memory_space=pltpu.HBM)
MIB = 1024 * 1024


def dot(a, b):
    return jnp.dot(a, b, preferred_element_type=F32)


def dot_t(a, b):
    return lax.dot_general(a, b, (((1,), (1,)), ((), ())), preferred_element_type=F32)


def cosine(x):
    turns = jnp.floor(x * (0.5 / math.pi) + 0.5)
    rest = (x - turns * 6.28125) - turns * (2.0 * math.pi - 6.28125)
    square = rest * rest
    value = jnp.full_like(square, 1.0 / math.factorial(16))
    for order in range(14, -2, -2):
        sign = 1.0 if order % 4 == 0 else -1.0
        value = value * square + sign / math.factorial(order)
    return value


def sigmoid(x):
    return 0.5 * jnp.tanh(0.5 * x) + 0.5


def floor_div(x, n):
    return jnp.floor((x + 0.5) * (1.0 / n))


def columns(row):
    parts = []
    for start in range(0, row.shape[1], LANES):
        part = jnp.broadcast_to(row[:, start : start + LANES], (LANES, LANES))
        parts.append(part.T)
    return jnp.concatenate(parts, axis=0)


def one_hot(column, width):
    lane = lax.broadcasted_iota(jnp.int32, column.shape, 1).astype(F32)
    parts = [(column - start == lane).astype(F32).astype(BF) for start in range(0, width, LANES)]
    return jnp.concatenate(parts, axis=1)


def one_hot_rows(row, height):
    line = lax.broadcasted_iota(jnp.int32, (height, row.shape[1]), 0).astype(F32)
    return (line == row).astype(F32)


def lanes(row):
    return jnp.concatenate([row, jnp.zeros((1, LANES - row.shape[1]), row.dtype)], axis=1)


def fetch(pairs, sems):
    copies = [pltpu.make_async_copy(a, b, sems.at[i]) for i, (a, b) in enumerate(pairs)]
    for copy in copies:
        copy.start()
    return copies


def serve_kernel(serve_hbm, memory_hbm, rows_ref, serve, memory, sems):
    copies = fetch([(serve_hbm, serve), (memory_hbm, memory)], sems)
    copies[0].wait()
    picks = one_hot(columns(serve[...].astype(F32)), memory.shape[0])
    copies[1].wait()
    rows_ref[...] = dot(picks, memory[...]).astype(BF)


def prepare_kernel(
    enc_width,
    sizes,
    scalar_ref,
    serve_hbm,
    time_hbm,
    stamp_hbm,
    edge_hbm,
    slot_hbm,
    lookup_hbm,
    freq_hbm,
    phase_hbm,
    tau_ref,
    swap_ref,
    sent_ref,
    near_ref,
    away_ref,
    serve,
    time,
    stamp,
    edge,
    slot,
    lookup,
    freq,
    phase,
    column,
    sems,
):
    copies = fetch(
        [
            (serve_hbm, serve),
            (time_hbm, time),
            (stamp_hbm, stamp),
            (edge_hbm, edge),
            (slot_hbm, slot),
            (lookup_hbm, lookup),
            (freq_hbm, freq),
            (phase_hbm, phase),
        ],
        sems,
    )
    for copy in copies:
        copy.wait()
    column[...] = columns(lookup[...].astype(F32))
    of_half(scalar_ref[0], column, near_ref, *sizes)
    of_half(1 - scalar_ref[0], column, away_ref, *sizes)
    picks = one_hot(columns(serve[...].astype(F32)), time.shape[1]).astype(F32)
    tau = jnp.sum(picks * time[...].astype(F32), axis=1, keepdims=True)
    slots = serve.shape[1]
    tau_ref[:slots, :] = jnp.broadcast_to(tau, (slots, LANES))
    tau_ref[slots : slots + 8, :] = jnp.broadcast_to(lanes(freq[...]), (8, LANES))
    tau_ref[slots + 8 : slots + 16, :] = jnp.broadcast_to(lanes(phase[...]), (8, LANES))
    first, second = (
        one_hot_rows(slot[c : c + 1, :].astype(F32), swap_ref.shape[0]) for c in range(2)
    )
    ends = jnp.concatenate([first, second], axis=1).astype(BF)
    others = jnp.concatenate([second, first], axis=1).astype(BF)
    swap_ref[...] = dot_t(ends, others).astype(BF)
    edges = edge.shape[0]
    first_edges = LANES - enc_width
    rest = edges - first_edges
    line = lax.broadcasted_iota(jnp.int32, (LANES, edges), 0)
    entry = lax.broadcasted_iota(jnp.int32, (LANES, edges), 1)
    wanted = jnp.where(line >= enc_width, line - enc_width, line + first_edges)
    shown = (line >= enc_width) | (line < rest)
    spread = ((wanted == entry) & shown).astype(F32).astype(BF)
    extra = dot(spread, edge[...])
    stamps = stamp[...].astype(F32)
    high = floor_div(stamps, 8)
    line = lax.broadcasted_iota(jnp.int32, extra.shape, 0)
    extra = jnp.where(line == rest, high, extra)
    extra = jnp.where(line == rest + 1, stamps - 8.0 * high, extra)
    sent_ref[...] = dot_t((first + second).astype(BF), extra.astype(BF)).astype(BF)


def of_half(half, column, rows_ref, ev_size, low_size, rest_size):
    block = column.shape[0] // (ev_size * 2 * low_size * rest_size)
    parts = []
    for e in range(ev_size):
        for r in range(rest_size):
            for w in range(low_size):
                start = ((2 * e + half) * low_size + w) * rest_size + r
                parts.append(column[pl.ds(pl.multiple_of(start * block, 8), block), :])
    joined = jnp.concatenate(parts, axis=0)
    for i in range(rows_ref.shape[0]):
        rows_ref[i : i + 1, :] = joined[i * LANES : (i + 1) * LANES, :].T[:1, :]


def flat_columns(rows_ref, begin, end):
    return jnp.concatenate([columns(rows_ref[i : i + 1, :]) for i in range(begin, end)], axis=0)


def partner_kernel(swap_ref, sent_ref, fetched_ref, out_ref):
    width = fetched_ref.shape[1]
    out_ref[:, :width] = dot(swap_ref[...], fetched_ref[...]).astype(BF)
    out_ref[:, width:] = sent_ref[...]


def update_kernel(
    enc_width,
    edge_width,
    shared,
    scalar_ref,
    hub_ref,
    serve_hbm,
    memory_hbm,
    bias_hbm,
    own_weight_hbm,
    tau_ref,
    near_ref,
    away_ref,
    message_ref,
    *refs,
):
    count = 6 if shared else 1
    weight_refs, refs = refs[:count], refs[count:]
    new_hbm, extended_hbm, rows_hbm, serve, memory_ref, bias, own_weight = refs[:7]
    pre, hid, out, rows_out, sems = refs[7:]
    pairs = [(serve_hbm, serve), (memory_hbm, memory_ref), (bias_hbm, bias)]
    pairs += [(own_weight_hbm, own_weight)] if shared else []
    copies = fetch(pairs, sems)
    nodes, width = memory_ref.shape
    slots = message_ref.shape[0]
    lane = lax.broadcasted_iota(jnp.int32, (slots, LANES), 1)
    rest = enc_width + edge_width - LANES
    extra = message_ref[:, width:].astype(F32)
    stamp = extra[:, rest : rest + 1] * 8.0 + extra[:, rest + 1 : rest + 2]
    gap = stamp - tau_ref[:slots, :]
    enc = cosine(gap * tau_ref[slots : slots + 1, :] + tau_ref[slots + 8 : slots + 9, :])
    mixed = jnp.where(lane < enc_width, enc, extra).astype(BF)
    tail = jnp.where(lane < rest, extra, 0.0).astype(BF)
    messages = jnp.concatenate([message_ref[:, :width], mixed, tail], axis=1)
    copies[0].wait()
    match = one_hot_rows(serve[...].astype(F32), nodes)
    counts = jnp.sum(match, axis=1, keepdims=True)
    summed = dot(match.astype(BF), messages)
    averaged = (summed / jnp.maximum(counts, 1.0)).astype(BF)
    copies[1].wait()
    memory = memory_ref[...]
    msg_width = 2 * width + enc_width + edge_width
    base = 2 * width + LANES
    left = jnp.concatenate([memory, averaged], axis=1)[:, :msg_width]
    hid_left = jnp.concatenate([jnp.zeros((nodes, rest), BF), memory], axis=1)
    piece = pre.shape[2]

    def whole(number, weight_ref):
        for start in range(0, weight_ref.shape[1], piece):
            cols = slice(start, start + piece)
            where = scalar_ref[number]
            pre[where] = dot(left, weight_ref[:msg_width, cols])
            hid[where] = dot(hid_left, weight_ref[base : base + rest + width, cols])
            number += 1

    if shared:
        for number, (mine, other, lower) in ((3, weight_refs[:3]), (4, weight_refs[3:])):
            where = scalar_ref[number]
            side = scalar_ref[5]
            halves = [left[:, :SHARED], left[:, SHARED:DIRECT]]
            first = jnp.where(side == 0, halves[0], halves[1])
            second = jnp.where(side == 0, halves[1], halves[0])
            pre[where] = (
                dot(first, mine[...])
                + dot(second, other[...])
                + dot(left[:, DIRECT:], lower[: msg_width - DIRECT, :])
            )
            hid[where] = dot(hid_left, lower[base - DIRECT :, :])
        copies[3].wait()
        whole(1, own_weight)
    else:
        whole(1, weight_refs[0])
    copies[2].wait()

    def third(ref, row, index):
        parts = []
        at, end = index * width, (index + 1) * width
        while at < end:
            inside = at % piece
            size = min(piece - inside, end - at)
            parts.append(ref[at // piece, :, inside : inside + size])
            at += size
        joined = parts[0] if len(parts) == 1 else jnp.concatenate(parts, axis=1)
        return joined + bias[row : row + 1, index * width : end]

    reset = sigmoid(third(pre, 0, 0) + third(hid, 1, 0))
    keep = sigmoid(third(pre, 0, 1) + third(hid, 1, 1))
    fresh = jnp.tanh(third(pre, 0, 2) + reset * third(hid, 1, 2))
    previous = memory.astype(F32)
    fresh = (1.0 - keep) * fresh + keep * previous
    new = jnp.where(counts > 0.0, fresh, previous).astype(BF)
    out[:nodes, :] = new
    line = lax.broadcasted_iota(jnp.int32, (16, nodes), 0)
    entry = lax.broadcasted_iota(jnp.int32, (16, nodes), 1)
    hub = ((entry == hub_ref[0]) & (line == 0)).astype(F32).astype(BF)
    out[nodes:, :] = dot(hub, new).astype(BF)
    for begin in range(0, away_ref.shape[0], 8):
        end = min(begin + 8, away_ref.shape[0])
        some = away_ref[begin:end, :]
        if end - begin < 8:
            some = jnp.concatenate([some, jnp.zeros((8 + begin - end, LANES), F32)], axis=0)
        out[nodes + 8 :, begin * 16 : begin * 16 + LANES] = some.astype(BF)
    sends = [
        pltpu.make_async_copy(out, extended_hbm, sems.at[0]),
        pltpu.make_async_copy(out.at[:nodes, :], new_hbm, sems.at[1]),
    ]
    for send in sends:
        send.start()
    count = near_ref.shape[0]
    for i, (begin, end) in enumerate(((0, count // 2), (count // 2, count))):
        some = slice(begin * LANES, end * LANES)
        rows_out[some, :] = dot(one_hot(flat_columns(near_ref, begin, end), nodes), new).astype(BF)
        sends.append(pltpu.make_async_copy(rows_out.at[some, :], rows_hbm.at[some, :], sems.at[2 + i]))
        sends[-1].start()
    for send in sends:
        send.wait()


def far_kernel(own_hbm, other_ref, out_ref, hub, sems):
    nodes = other_ref.shape[0] - 16
    copies = fetch([(own_hbm.at[nodes:, :], hub)], sems)
    count = out_ref.shape[0] * (out_ref.shape[1] - 8) // LANES
    wanted = other_ref[nodes:, :].astype(F32)[8:, :]
    index = [wanted[i % 8 : i % 8 + 1, i // 8 * LANES : (i // 8 + 1) * LANES] for i in range(count)]
    picks = one_hot(jnp.concatenate([columns(row) for row in index], axis=0), nodes)
    rows = dot(picks, other_ref[:nodes, :])
    near, block, width = out_ref.shape
    out_ref[:, : block - 8, :] = rows.reshape(near, block - 8, width).astype(BF)
    copies[0].wait()
    hubs = jnp.concatenate(
        [other_ref[nodes : nodes + 1, :], hub[0:1, :], jnp.zeros((6, width), BF)], axis=0
    )
    out_ref[:, block - 8 :, :] = jnp.broadcast_to(hubs[None], (near, 8, width))


def places(slot, hi, cap, low_size, rest_size):
    owner = floor_div(slot, cap)
    line = floor_div(owner, rest_size)
    rest = owner - rest_size * line
    half = floor_div(line, low_size)
    ev = floor_div(half, 2)
    relay = (ev * rest_size + rest) * low_size + line - low_size * half
    return relay, half - 2.0 * ev == hi, slot - cap * owner


def picks_of(index, width):
    return jnp.concatenate(
        [one_hot(columns(index[k : k + 1, :]), width) for k in range(index.shape[0])], axis=0
    )


def pick_kernel(
    cap,
    sizes,
    scalar_ref,
    slot_hbm,
    hub_hbm,
    gap_hbm,
    freq_hbm,
    phase_hbm,
    looked_ref,
    picked_ref,
    far_ref,
    hub_ref,
    enc_ref,
    own_ref,
    slot,
    hub,
    gaps,
    freq,
    phase,
    sems,
):
    copies = fetch(
        [(slot_hbm, slot), (hub_hbm, hub), (gap_hbm, gaps), (freq_hbm, freq), (phase_hbm, phase)],
        sems,
    )
    for copy in copies:
        copy.wait()
    owners, block, width = looked_ref.shape
    hi = scalar_ref[0].astype(F32)
    relay, near, place = places(slot[...].astype(F32), hi, cap, *sizes)
    index = jnp.where(near, relay * block + place, -1.0)
    looked = looked_ref[...].reshape(owners * block, width)
    events = gaps.shape[1]
    picks = [one_hot(columns(index[k : k + 1, :]), owners * block) for k in range(slot.shape[0])]
    picked_ref[...] = dot(jnp.concatenate(picks, axis=0), looked).astype(BF)
    far_ref[...] = jnp.where(near, -1.0, relay * (block + 8) + place)
    relay, near, place = places(hub[...].astype(F32), hi, 1, *sizes)
    hub_ref[...] = relay * 8.0 + jnp.where(near, 1.0, 0.0)
    freq_row, phase_row = lanes(freq[...]), lanes(phase[...])
    for k in range(gaps.shape[0]):
        angle = columns(gaps[k : k + 1, :].astype(F32)) * freq_row + phase_row
        enc_ref[k * events : (k + 1) * events, :] = cosine(angle).astype(BF)
    own_ref[...] = jnp.broadcast_to(cosine(phase_row), (8, LANES)).astype(BF)


def attend_kernel(
    keyval_hbm,
    enc_hbm,
    query_hbm,
    output_hbm,
    picked_ref,
    far_ref,
    hub_ref,
    own_enc_ref,
    looked_ref,
    out_ref,
    keyval_ref,
    enc_ref,
    query_ref,
    output_ref,
    sems,
):
    copies = fetch(
        [
            (keyval_hbm, keyval_ref),
            (enc_hbm, enc_ref),
            (query_hbm, query_ref),
            (output_hbm, output_ref),
        ],
        sems,
    )
    owners, block, width = looked_ref.shape
    events = out_ref.shape[0]
    near = enc_ref.shape[0] // events
    att = query_ref.shape[1]
    head = att // HEADS
    looked = looked_ref[...].reshape(owners * block, width)
    hub_rows = looked_ref[:, block - 8 :, :].reshape(owners * 8, width)
    hub_near = dot(picks_of(hub_ref[...], owners * 8), hub_rows).astype(BF)
    picks = picks_of(far_ref[...], owners * block)
    rows = (dot(picks, looked) + picked_ref[...].astype(F32)).astype(BF)
    own = rows[:events]
    near_rows = jnp.concatenate([rows[events:], hub_near], axis=0)
    copies[0].wait()
    copies[1].wait()
    key_width = keyval_ref.shape[0]
    key_input = jnp.concatenate([near_rows, enc_ref[...]], axis=1)[:, :key_width]
    keyval = dot(key_input, keyval_ref[...]).astype(BF).astype(F32)
    copies[2].wait()
    own_enc = jnp.broadcast_to(own_enc_ref[0:1, :], (events, LANES))
    query_input = jnp.concatenate([own, own_enc], axis=1)[:, :key_width]
    query = dot(query_input, query_ref[...]).astype(BF).astype(F32)
    mixed = []
    for h in range(HEADS):
        cols = slice(h * head, (h + 1) * head)
        vals = slice(att + h * head, att + (h + 1) * head)
        slabs = [slice(k * events, (k + 1) * events) for k in range(near)]
        scores = [
            jnp.sum(query[:, cols] * keyval[s, cols], axis=1, keepdims=True) * head**-0.5
            for s in slabs
        ]
        top = functools.reduce(jnp.maximum, scores)
        expo = [jnp.exp(s - top) for s in scores]
        total = functools.reduce(jnp.add, expo)
        prob = [(e / total).astype(BF).astype(F32) for e in expo]
        mixed.append(sum(p * keyval[s, vals] for p, s in zip(prob, slabs)))
    joined = jnp.concatenate([m.astype(BF) for m in mixed] + [own], axis=1)
    copies[3].wait()
    out_ref[...] = dot(joined, output_ref[...]).astype(BF)


def exchange(x, axes):
    return lax.all_to_all(x, axes, split_axis=0, concat_axis=0, tiled=True)


def after(x, *earlier):
    return lax.optimization_barrier((x, *earlier))[0]


def call(kernel, name, out_shape, smem, hbm, vmem, fetched=(), scratch=(), left=(), kept=(), limit=20, extra_sems=0, flops=0):
    many = isinstance(out_shape, tuple)
    specs = tuple(HBM if x in left else VMEM for x in range(len(out_shape))) if many else VMEM
    copies = [pltpu.VMEM(x.shape, x.dtype) for x in fetched]
    sems = [pltpu.SemaphoreType.DMA((len(fetched) + extra_sems,))] if fetched else []
    return pl.pallas_call(
        kernel,
        out_shape=out_shape,
        in_specs=[SMEM] * len(smem) + [HBM] * len(hbm) + [VMEM] * (len(kept) + len(vmem)),
        out_specs=specs,
        scratch_shapes=copies + list(scratch) + sems,
        compiler_params=pltpu.CompilerParams(vmem_limit_bytes=limit * MIB),
        name=name,
        cost_estimate=pl.CostEstimate(flops=flops, bytes_accessed=0, transcendentals=0) if flops else None,
    )(*smem, *[pltpu.with_memory_space_constraint(x, pltpu.HBM) for x in hbm], *[pltpu.with_memory_space_constraint(x, pltpu.VMEM) for x in kept], *vmem)


def cores_share(gru_weight):
    half = gru_weight.shape[1] // 2
    return lax.axis_size("ev") == 2 and lax.axis_size("rest") % 4 == 0 and half % LANES == 0


def other_ev(x):
    return lax.ppermute(x, "ev", [(0, 1), (1, 0)])


def other_x(x):
    return lax.ppermute(x, "rest", [(i, i ^ 2) for i in range(lax.axis_size("rest"))])


def other_core(x):
    return lax.ppermute(x, "rest", [(i, i ^ 1) for i in range(lax.axis_size("rest"))])


def other_half(x):
    return lax.ppermute(x, "hi", [(0, 1), (1, 0)])


def local(
    memory,
    last_time,
    event_time,
    edge_features,
    update_slot,
    update_serve,
    lookup_slot,
    lookup_serve,
    neighbour_gap,
    hub_node,
    hub_choice,
    time_freq,
    time_phase,
    gru_weight,
    gru_bias,
    query_weight,
    keyval_weight,
    output_weight,
):
    ev_size, hi_size, low_size, rest_size = (lax.axis_size(a) for a in BOTH)
    ev, hi, _, rest_index = (lax.axis_index(a) for a in BOTH)
    near = ev_size * low_size * rest_size
    devices = hi_size * near
    sizes = (ev_size, low_size, rest_size)
    nodes, width = memory.shape
    events = event_time.shape[0]
    slots = update_serve.shape[1]
    cap = slots // devices
    cap_lookup = lookup_serve.shape[1] // devices
    block = -(-cap_lookup // 8) * 8
    enc_width = time_freq.shape[0]
    edge_width = edge_features.shape[1]
    freq, phase = time_freq[None, :], time_phase[None, :]
    shape, sent_shape = jax.ShapeDtypeStruct, pltpu.HBM

    shared = cores_share(gru_weight)
    total, half = gru_weight.shape[0], gru_weight.shape[1] // 2
    rows = call(
        serve_kernel,
        "serve_endpoints",
        sent_shape((slots, width), BF),
        (),
        (update_serve, memory),
        (),
        fetched=(update_serve, memory),
    )
    if shared:
        late_weight = after(gru_weight, rows)
        side, column_at = rest_index // 2 % 2, rest_index % 2 * half
        first = other_ev(
            lax.dynamic_slice(late_weight, (side * SHARED, column_at), (SHARED, half))
        )
        piece = half
        core, other = rest_index % 2, 2 * (1 - ev)
        place = [2 * ev, 2 * ev + 1, other + core, other + 1 - core]
    else:
        whole = lax.all_gather(gru_weight, "ev", axis=1, tiled=True)
        piece, place = whole.shape[1], [jnp.int32(0)]
    scalars = jnp.stack([hi] + place + [rest_index // 2 % 2]).astype(jnp.int32)
    fetched = exchange(rows.reshape(devices, cap, width), BOTH).reshape(slots, width)

    lookup_row = lookup_serve
    if block != cap_lookup:
        lookup_row = jnp.pad(
            lookup_serve.reshape(devices, cap_lookup),
            ((0, 0), (0, block - cap_lookup)),
            constant_values=-1,
        ).reshape(1, devices * block)
    raw = (
        after(update_serve, rows),
        last_time[None, :],
        event_time[None, :],
        edge_features.T,
        update_slot.T,
        lookup_row,
        freq,
        phase,
    )
    rows_shape = pltpu.VMEM((near * block // LANES, LANES), F32)
    tau, swap, sent, near_index, away_index = call(
        functools.partial(prepare_kernel, enc_width, sizes),
        "prepare",
        (
            pltpu.VMEM((slots + 16, LANES), F32),
            pltpu.VMEM((slots, slots), BF),
            pltpu.VMEM((slots, LANES), BF),
            rows_shape,
            rows_shape,
        ),
        (scalars,),
        raw,
        (),
        fetched=raw,
        scratch=(pltpu.VMEM((devices * block, LANES), F32),),
    )
    if shared:
        sent = after(sent, first)
    message = call(
        partner_kernel,
        "partner_rows",
        sent_shape((slots, width + LANES), BF),
        (),
        (),
        (fetched,),
        kept=(swap, sent),
    )
    if shared:
        late_weight = after(gru_weight, rows)
        lower = other_ev(lax.dynamic_slice(late_weight, (DIRECT, column_at), (total - DIRECT, half)))
        first = after(first, message)
        second = other_x(first)
        pieces = [first, second, after(lower, second)]
        pieces += [other_core(x) for x in pieces]
    else:
        pieces = [whole]
    message = exchange(message.reshape(devices, cap, width + LANES), BOTH)
    raw = (update_serve, memory, gru_bias, gru_weight)
    parts = pltpu.VMEM((3 * width // piece, nodes, piece), F32)
    new_memory, extended, near_rows = call(
        functools.partial(update_kernel, enc_width, edge_width, shared),
        "update_memory",
        (
            sent_shape((nodes, width), BF),
            sent_shape((nodes + 16, width), BF),
            sent_shape((near * block, width), BF),
        ),
        (scalars, hub_node),
        raw,
        (message.reshape(slots, width + LANES), *pieces),
        kept=(tau, near_index, away_index),
        fetched=raw,
        scratch=(
            parts,
            parts,
            pltpu.VMEM((nodes + 16, width), BF),
            pltpu.VMEM((near * block, width), BF),
        ),
        left=(0, 1, 2),
        limit=28,
    )
    other_extended = other_half(extended)
    near_looked = exchange(near_rows.reshape(near, block, width), NEAR)
    far_rows = call(
        far_kernel,
        "far_rows",
        sent_shape((near, block + 8, width), BF),
        (),
        (extended,),
        (other_extended,),
        fetched=(shape((16, width), BF),),
        flops=3 * 10**10,
    )
    far_looked = exchange(far_rows, NEAR)
    raw = (lookup_slot.T, hub_choice.T, neighbour_gap.T, freq, phase)
    routes, near_count = lookup_slot.shape[1] * events, neighbour_gap.shape[1] * events
    picked, pick_far, pick_hub, enc, own_enc = call(
        functools.partial(pick_kernel, cap_lookup, sizes[1:]),
        "pick_near",
        (
            pltpu.VMEM((routes, width), BF),
            pltpu.VMEM(lookup_slot.T.shape, F32),
            pltpu.VMEM(hub_choice.T.shape, F32),
            sent_shape((near_count, LANES), BF),
            pltpu.VMEM((8, LANES), BF),
        ),
        (scalars,),
        raw,
        (near_looked,),
        fetched=raw,
    )
    raw = (keyval_weight, enc, query_weight, output_weight)
    embedding = call(
        attend_kernel,
        "attend",
        sent_shape((events, width), BF),
        (),
        raw,
        (far_looked,),
        kept=(picked, pick_far, pick_hub, own_enc),
        fetched=raw,
    )
    return (new_memory, embedding)


def solution(mesh):
    ev_size, mem_size = mesh.devices.shape
    split = jax.sharding.Mesh(mesh.devices.reshape(ev_size, 2, 2, mem_size // 4), BOTH)
    both = P(BOTH)
    rows = P(BOTH, None)
    return jax.shard_map(
        local,
        mesh=split,
        in_specs=(
            rows,
            both,
            both,
            rows,
            rows,
            rows,
            rows,
            rows,
            rows,
            both,
            rows,
            P(),
            P(),
            P(None, "ev"),
            P(),
            P(),
            P(),
            P(),
        ),
        out_specs=(rows, rows),
        check_vma=False,
    )
```

```python
import functools
import math

import jax
import jax.numpy as jnp
from jax import lax
from jax.experimental import pallas as pl
from jax.experimental.pallas import tpu as pltpu
from jax.sharding import PartitionSpec as P

HEADS = 2
LANES = 128
SHARED = 384
DIRECT = 2 * SHARED
BF = jnp.bfloat16
F32 = jnp.float32
BOTH = ("ev", "hi", "low", "rest")
NEAR = ("ev", "rest", "low")
VMEM = pl.BlockSpec(memory_space=pltpu.VMEM)
SMEM = pl.BlockSpec(memory_space=pltpu.SMEM)
HBM = pl.BlockSpec(memory_space=pltpu.HBM)
MIB = 1024 * 1024


def dot(a, b):
    return jnp.dot(a, b, preferred_element_type=F32)


def dot_t(a, b):
    return lax.dot_general(a, b, (((1,), (1,)), ((), ())), preferred_element_type=F32)


def cosine(x):
    turns = jnp.floor(x * (0.5 / math.pi) + 0.5)
    rest = (x - turns * 6.28125) - turns * (2.0 * math.pi - 6.28125)
    square = rest * rest
    value = jnp.full_like(square, 1.0 / math.factorial(16))
    for order in range(14, -2, -2):
        sign = 1.0 if order % 4 == 0 else -1.0
        value = value * square + sign / math.factorial(order)
    return value


def sigmoid(x):
    return 0.5 * jnp.tanh(0.5 * x) + 0.5


def floor_div(x, n):
    return jnp.floor((x + 0.5) * (1.0 / n))


def columns(row):
    parts = []
    for start in range(0, row.shape[1], LANES):
        part = jnp.broadcast_to(row[:, start : start + LANES], (LANES, LANES))
        parts.append(part.T)
    return jnp.concatenate(parts, axis=0)


def one_hot(column, width):
    lane = lax.broadcasted_iota(jnp.int32, column.shape, 1).astype(F32)
    parts = [(column - start == lane).astype(F32).astype(BF) for start in range(0, width, LANES)]
    return jnp.concatenate(parts, axis=1)


def one_hot_rows(row, height):
    line = lax.broadcasted_iota(jnp.int32, (height, row.shape[1]), 0).astype(F32)
    return (line == row).astype(F32)


def lanes(row):
    return jnp.concatenate([row, jnp.zeros((1, LANES - row.shape[1]), row.dtype)], axis=1)


def fetch(pairs, sems):
    copies = [pltpu.make_async_copy(a, b, sems.at[i]) for i, (a, b) in enumerate(pairs)]
    for copy in copies:
        copy.start()
    return copies


def serve_kernel(serve_hbm, memory_hbm, rows_ref, serve, memory, sems):
    copies = fetch([(serve_hbm, serve), (memory_hbm, memory)], sems)
    copies[0].wait()
    picks = one_hot(columns(serve[...].astype(F32)), memory.shape[0])
    copies[1].wait()
    rows_ref[...] = dot(picks, memory[...]).astype(BF)


def prepare_kernel(
    enc_width,
    sizes,
    scalar_ref,
    serve_hbm,
    time_hbm,
    stamp_hbm,
    edge_hbm,
    slot_hbm,
    lookup_hbm,
    freq_hbm,
    phase_hbm,
    tau_ref,
    swap_ref,
    sent_ref,
    near_ref,
    away_ref,
    serve,
    time,
    stamp,
    edge,
    slot,
    lookup,
    freq,
    phase,
    column,
    sems,
):
    copies = fetch(
        [
            (serve_hbm, serve),
            (time_hbm, time),
            (stamp_hbm, stamp),
            (edge_hbm, edge),
            (slot_hbm, slot),
            (lookup_hbm, lookup),
            (freq_hbm, freq),
            (phase_hbm, phase),
        ],
        sems,
    )
    for copy in copies:
        copy.wait()
    column[...] = columns(lookup[...].astype(F32))
    of_half(scalar_ref[0], column, near_ref, *sizes)
    of_half(1 - scalar_ref[0], column, away_ref, *sizes)
    picks = one_hot(columns(serve[...].astype(F32)), time.shape[1]).astype(F32)
    tau = jnp.sum(picks * time[...].astype(F32), axis=1, keepdims=True)
    slots = serve.shape[1]
    tau_ref[:slots, :] = jnp.broadcast_to(tau, (slots, LANES))
    tau_ref[slots : slots + 8, :] = jnp.broadcast_to(lanes(freq[...]), (8, LANES))
    tau_ref[slots + 8 : slots + 16, :] = jnp.broadcast_to(lanes(phase[...]), (8, LANES))
    first, second = (
        one_hot_rows(slot[c : c + 1, :].astype(F32), swap_ref.shape[0]) for c in range(2)
    )
    ends = jnp.concatenate([first, second], axis=1).astype(BF)
    others = jnp.concatenate([second, first], axis=1).astype(BF)
    swap_ref[...] = dot_t(ends, others).astype(BF)
    edges = edge.shape[0]
    first_edges = LANES - enc_width
    rest = edges - first_edges
    line = lax.broadcasted_iota(jnp.int32, (LANES, edges), 0)
    entry = lax.broadcasted_iota(jnp.int32, (LANES, edges), 1)
    wanted = jnp.where(line >= enc_width, line - enc_width, line + first_edges)
    shown = (line >= enc_width) | (line < rest)
    spread = ((wanted == entry) & shown).astype(F32).astype(BF)
    extra = dot(spread, edge[...])
    stamps = stamp[...].astype(F32)
    high = floor_div(stamps, 8)
    line = lax.broadcasted_iota(jnp.int32, extra.shape, 0)
    extra = jnp.where(line == rest, high, extra)
    extra = jnp.where(line == rest + 1, stamps - 8.0 * high, extra)
    sent = dot_t((first + second).astype(BF), extra.astype(BF))
    if len(sent_ref.shape) == 3:
        sent = sent.reshape(sent_ref.shape[0], -1, LANES)
        lines = sent_ref.shape[1]
        sent = sent[:, :lines, :] + half_turn(sent[:, lines:, :])
    sent_ref[...] = sent.astype(BF)


def of_half(half, column, rows_ref, ev_size, low_size, rest_size):
    block = column.shape[0] // (ev_size * 2 * low_size * rest_size)
    parts = []
    for e in range(ev_size):
        for r in range(rest_size):
            for w in range(low_size):
                start = ((2 * e + half) * low_size + w) * rest_size + r
                parts.append(column[pl.ds(pl.multiple_of(start * block, 8), block), :])
    joined = jnp.concatenate(parts, axis=0)
    for i in range(rows_ref.shape[0]):
        rows_ref[i : i + 1, :] = joined[i * LANES : (i + 1) * LANES, :].T[:1, :]


def flat_columns(rows_ref, begin, end):
    return jnp.concatenate([columns(rows_ref[i : i + 1, :]) for i in range(begin, end)], axis=0)


def half_turn(x):
    return jnp.concatenate([x[..., LANES // 2 :], x[..., : LANES // 2]], axis=x.ndim - 1)


def partner_kernel(swap_ref, sent_ref, fetched_ref, out_ref):
    width = fetched_ref.shape[1]
    rows = dot(swap_ref[...], fetched_ref[...])
    if len(out_ref.shape) == 3:
        to_chunks(rows, out_ref)
        out_ref[:, out_ref.shape[1] - sent_ref.shape[1] :, :] = sent_ref[...]
    else:
        out_ref[:, :width] = rows.astype(BF)
        out_ref[:, width:] = sent_ref[...]


def to_chunks(rows, out_ref):
    blocks = out_ref.shape[0]
    lines = rows.shape[0] // blocks
    for c in range(rows.shape[1] // LANES):
        chunk = rows[:, c * LANES : (c + 1) * LANES].reshape(blocks, lines, LANES)
        out_ref[:, c * lines : (c + 1) * lines, :] = chunk.astype(BF)


def from_chunks(ref, lines, count):
    blocks = ref.shape[0]
    chunks = [
        ref[:, c * lines : (c + 1) * lines, :].reshape(blocks * lines, LANES) for c in range(count)
    ]
    return jnp.concatenate(chunks, axis=1)


def update_kernel(
    enc_width,
    edge_width,
    shared,
    scalar_ref,
    hub_ref,
    serve_hbm,
    memory_hbm,
    bias_hbm,
    own_weight_hbm,
    tau_ref,
    near_ref,
    away_ref,
    message_ref,
    *refs,
):
    count = 6 if shared else 1
    weight_refs, refs = refs[:count], refs[count:]
    new_hbm, extended_hbm, rows_hbm, serve, memory_ref, bias, own_weight = refs[:7]
    pre, hid, out, rows_out, sems = refs[7:]
    pairs = [(serve_hbm, serve), (memory_hbm, memory_ref), (bias_hbm, bias)]
    pairs += [(own_weight_hbm, own_weight)] if shared else []
    copies = fetch(pairs, sems)
    nodes, width = memory_ref.shape
    slots = serve.shape[1]
    lane = lax.broadcasted_iota(jnp.int32, (slots, LANES), 1)
    rest = enc_width + edge_width - LANES
    if len(message_ref.shape) == 3:
        lines = slots // message_ref.shape[0]
        chunks = width // LANES
        partner = from_chunks(message_ref, lines, chunks)
        extra = message_ref[:, chunks * lines :, :].astype(F32)
        extra = jnp.concatenate([extra, half_turn(extra)], axis=1).reshape(slots, LANES)
    else:
        partner = message_ref[:, :width]
        extra = message_ref[:, width:].astype(F32)
    stamp = extra[:, rest : rest + 1] * 8.0 + extra[:, rest + 1 : rest + 2]
    gap = stamp - tau_ref[:slots, :]
    enc = cosine(gap * tau_ref[slots : slots + 1, :] + tau_ref[slots + 8 : slots + 9, :])
    mixed = jnp.where(lane < enc_width, enc, extra).astype(BF)
    tail = jnp.where(lane < rest, extra, 0.0).astype(BF)
    messages = jnp.concatenate([partner, mixed, tail], axis=1)
    copies[0].wait()
    match = one_hot_rows(serve[...].astype(F32), nodes)
    counts = jnp.sum(match, axis=1, keepdims=True)
    summed = dot(match.astype(BF), messages)
    averaged = (summed / jnp.maximum(counts, 1.0)).astype(BF)
    copies[1].wait()
    memory = memory_ref[...]
    msg_width = 2 * width + enc_width + edge_width
    base = 2 * width + LANES
    left = jnp.concatenate([memory, averaged], axis=1)[:, :msg_width]
    hid_left = jnp.concatenate([jnp.zeros((nodes, rest), BF), memory], axis=1)
    piece = pre.shape[2]

    def whole(number, weight_ref):
        for start in range(0, weight_ref.shape[1], piece):
            cols = slice(start, start + piece)
            where = scalar_ref[number]
            pre[where] = dot(left, weight_ref[:msg_width, cols])
            hid[where] = dot(hid_left, weight_ref[base : base + rest + width, cols])
            number += 1

    if shared:
        for number, (mine, other, lower) in ((3, weight_refs[:3]), (4, weight_refs[3:])):
            where = scalar_ref[number]
            side = scalar_ref[5]
            halves = [left[:, :SHARED], left[:, SHARED:DIRECT]]
            first = jnp.where(side == 0, halves[0], halves[1])
            second = jnp.where(side == 0, halves[1], halves[0])
            pre[where] = (
                dot(first, mine[...])
                + dot(second, other[...])
                + dot(left[:, DIRECT:], lower[: msg_width - DIRECT, :])
            )
            hid[where] = dot(hid_left, lower[base - DIRECT :, :])
        copies[3].wait()
        whole(1, own_weight)
    else:
        whole(1, weight_refs[0])
    copies[2].wait()

    def third(ref, row, index):
        parts = []
        at, end = index * width, (index + 1) * width
        while at < end:
            inside = at % piece
            size = min(piece - inside, end - at)
            parts.append(ref[at // piece, :, inside : inside + size])
            at += size
        joined = parts[0] if len(parts) == 1 else jnp.concatenate(parts, axis=1)
        return joined + bias[row : row + 1, index * width : end]

    reset = sigmoid(third(pre, 0, 0) + third(hid, 1, 0))
    keep = sigmoid(third(pre, 0, 1) + third(hid, 1, 1))
    fresh = jnp.tanh(third(pre, 0, 2) + reset * third(hid, 1, 2))
    previous = memory.astype(F32)
    fresh = (1.0 - keep) * fresh + keep * previous
    new = jnp.where(counts > 0.0, fresh, previous).astype(BF)
    out[:nodes, :] = new
    line = lax.broadcasted_iota(jnp.int32, (16, nodes), 0)
    entry = lax.broadcasted_iota(jnp.int32, (16, nodes), 1)
    hub = ((entry == hub_ref[0]) & (line == 0)).astype(F32).astype(BF)
    out[nodes:, :] = dot(hub, new).astype(BF)
    for begin in range(0, away_ref.shape[0], 8):
        end = min(begin + 8, away_ref.shape[0])
        some = away_ref[begin:end, :]
        if end - begin < 8:
            some = jnp.concatenate([some, jnp.zeros((8 + begin - end, LANES), F32)], axis=0)
        out[nodes + 8 :, begin * 16 : begin * 16 + LANES] = some.astype(BF)
    sends = [
        pltpu.make_async_copy(out, extended_hbm, sems.at[0]),
        pltpu.make_async_copy(out.at[:nodes, :], new_hbm, sems.at[1]),
    ]
    for send in sends:
        send.start()
    count = near_ref.shape[0]
    for i, (begin, end) in enumerate(((0, count // 2), (count // 2, count))):
        some = slice(begin * LANES, end * LANES)
        rows_out[some, :] = dot(one_hot(flat_columns(near_ref, begin, end), nodes), new).astype(BF)
        sends.append(pltpu.make_async_copy(rows_out.at[some, :], rows_hbm.at[some, :], sems.at[2 + i]))
        sends[-1].start()
    for send in sends:
        send.wait()


def far_kernel(own_hbm, other_ref, out_ref, hub, sems):
    nodes, width = other_ref.shape[0] - 16, other_ref.shape[1]
    copies = fetch([(own_hbm.at[nodes:, :], hub)], sems)
    chunks = width // LANES
    near, lines, _ = out_ref.shape
    wanted = other_ref[nodes:, :].astype(F32)[8:, :]
    count = near * (lines - 8) // chunks // LANES
    index = [wanted[i % 8 : i % 8 + 1, i // 8 * LANES : (i // 8 + 1) * LANES] for i in range(count)]
    picks = one_hot(jnp.concatenate([columns(row) for row in index], axis=0), nodes)
    to_chunks(dot(picks, other_ref[:nodes, :]), out_ref)
    copies[0].wait()
    hubs = [other_ref[nodes : nodes + 1, :], hub[0:1, :]]
    parts = [h[:, c * LANES : (c + 1) * LANES].astype(F32) for h in hubs for c in range(chunks)]
    parts = jnp.concatenate(parts, axis=0).astype(BF)
    out_ref[:, lines - 8 :, :] = jnp.broadcast_to(parts[None], (near, 8, LANES))


def places(slot, hi, cap, low_size, rest_size):
    owner = floor_div(slot, cap)
    line = floor_div(owner, rest_size)
    rest = owner - rest_size * line
    half = floor_div(line, low_size)
    ev = floor_div(half, 2)
    relay = (ev * rest_size + rest) * low_size + line - low_size * half
    return relay, half - 2.0 * ev == hi, slot - cap * owner


def picks_of(index, width):
    return jnp.concatenate(
        [one_hot(columns(index[k : k + 1, :]), width) for k in range(index.shape[0])], axis=0
    )


def pick_kernel(
    cap,
    sizes,
    scalar_ref,
    slot_hbm,
    hub_hbm,
    gap_hbm,
    freq_hbm,
    phase_hbm,
    looked_ref,
    picked_ref,
    far_ref,
    hub_ref,
    enc_ref,
    own_ref,
    slot,
    hub,
    gaps,
    freq,
    phase,
    sems,
):
    copies = fetch(
        [(slot_hbm, slot), (hub_hbm, hub), (gap_hbm, gaps), (freq_hbm, freq), (phase_hbm, phase)],
        sems,
    )
    for copy in copies:
        copy.wait()
    owners, block, width = looked_ref.shape
    hi = scalar_ref[0].astype(F32)
    relay, near, place = places(slot[...].astype(F32), hi, cap, *sizes)
    index = jnp.where(near, relay * block + place, -1.0)
    looked = looked_ref[...].reshape(owners * block, width)
    events = gaps.shape[1]
    picks = [one_hot(columns(index[k : k + 1, :]), owners * block) for k in range(slot.shape[0])]
    picked_ref[...] = dot(jnp.concatenate(picks, axis=0), looked).astype(BF)
    far_ref[...] = jnp.where(near, -1.0, relay * block + place)
    relay, near, place = places(hub[...].astype(F32), hi, 1, *sizes)
    hub_ref[...] = relay * 8.0 + jnp.where(near, 4.0, 0.0)
    freq_row, phase_row = lanes(freq[...]), lanes(phase[...])
    for k in range(gaps.shape[0]):
        angle = columns(gaps[k : k + 1, :].astype(F32)) * freq_row + phase_row
        enc_ref[k * events : (k + 1) * events, :] = cosine(angle).astype(BF)
    own_ref[...] = jnp.broadcast_to(cosine(phase_row), (8, LANES)).astype(BF)


def attend_kernel(
    keyval_hbm,
    enc_hbm,
    query_hbm,
    output_hbm,
    picked_ref,
    far_ref,
    hub_ref,
    own_enc_ref,
    looked_ref,
    out_ref,
    keyval_ref,
    enc_ref,
    query_ref,
    output_ref,
    sems,
):
    copies = fetch(
        [
            (keyval_hbm, keyval_ref),
            (enc_hbm, enc_ref),
            (query_hbm, query_ref),
            (output_hbm, output_ref),
        ],
        sems,
    )
    events, width = out_ref.shape
    chunks = width // LANES
    owners = looked_ref.shape[0]
    block = (looked_ref.shape[1] - 8) // chunks
    near = enc_ref.shape[0] // events
    att = query_ref.shape[1]
    head = att // HEADS
    looked = from_chunks(looked_ref, block, chunks)
    hub_lines = looked_ref[:, chunks * block :, :].astype(F32).reshape(owners * 8, LANES)
    hub_rows = [hub_lines] + [
        jnp.concatenate([hub_lines[c:], hub_lines[:c]], axis=0) for c in range(1, chunks)
    ]
    hub_rows = jnp.concatenate(hub_rows, axis=1).astype(BF)
    hub_near = dot(picks_of(hub_ref[...], owners * 8), hub_rows).astype(BF)
    picks = picks_of(far_ref[...], owners * block)
    rows = (dot(picks, looked) + picked_ref[...].astype(F32)).astype(BF)
    own = rows[:events]
    near_rows = jnp.concatenate([rows[events:], hub_near], axis=0)
    copies[0].wait()
    copies[1].wait()
    key_width = keyval_ref.shape[0]
    key_input = jnp.concatenate([near_rows, enc_ref[...]], axis=1)[:, :key_width]
    keyval = dot(key_input, keyval_ref[...]).astype(BF).astype(F32)
    copies[2].wait()
    own_enc = jnp.broadcast_to(own_enc_ref[0:1, :], (events, LANES))
    query_input = jnp.concatenate([own, own_enc], axis=1)[:, :key_width]
    query = dot(query_input, query_ref[...]).astype(BF).astype(F32)
    mixed = []
    for h in range(HEADS):
        cols = slice(h * head, (h + 1) * head)
        vals = slice(att + h * head, att + (h + 1) * head)
        slabs = [slice(k * events, (k + 1) * events) for k in range(near)]
        scores = [
            jnp.sum(query[:, cols] * keyval[s, cols], axis=1, keepdims=True) * head**-0.5
            for s in slabs
        ]
        top = functools.reduce(jnp.maximum, scores)
        expo = [jnp.exp(s - top) for s in scores]
        total = functools.reduce(jnp.add, expo)
        prob = [(e / total).astype(BF).astype(F32) for e in expo]
        mixed.append(sum(p * keyval[s, vals] for p, s in zip(prob, slabs)))
    joined = jnp.concatenate([m.astype(BF) for m in mixed] + [own], axis=1)
    copies[3].wait()
    out_ref[...] = dot(joined, output_ref[...]).astype(BF)


def exchange(x, axes):
    return lax.all_to_all(x, axes, split_axis=0, concat_axis=0, tiled=True)


def after(x, *earlier):
    return lax.optimization_barrier((x, *earlier))[0]


def call(kernel, name, out_shape, smem, hbm, vmem, fetched=(), scratch=(), left=(), kept=(), limit=20, extra_sems=0, flops=0):
    many = isinstance(out_shape, tuple)
    specs = tuple(HBM if x in left else VMEM for x in range(len(out_shape))) if many else VMEM
    copies = [pltpu.VMEM(x.shape, x.dtype) for x in fetched]
    sems = [pltpu.SemaphoreType.DMA((len(fetched) + extra_sems,))] if fetched else []
    return pl.pallas_call(
        kernel,
        out_shape=out_shape,
        in_specs=[SMEM] * len(smem) + [HBM] * len(hbm) + [VMEM] * (len(kept) + len(vmem)),
        out_specs=specs,
        scratch_shapes=copies + list(scratch) + sems,
        compiler_params=pltpu.CompilerParams(vmem_limit_bytes=limit * MIB),
        name=name,
        cost_estimate=pl.CostEstimate(flops=flops, bytes_accessed=0, transcendentals=0) if flops else None,
    )(*smem, *[pltpu.with_memory_space_constraint(x, pltpu.HBM) for x in hbm], *[pltpu.with_memory_space_constraint(x, pltpu.VMEM) for x in kept], *vmem)


def cores_share(gru_weight):
    half = gru_weight.shape[1] // 2
    return lax.axis_size("ev") == 2 and lax.axis_size("rest") % 4 == 0 and half % LANES == 0


def other_ev(x):
    return lax.ppermute(x, "ev", [(0, 1), (1, 0)])


def other_x(x):
    return lax.ppermute(x, "rest", [(i, i ^ 2) for i in range(lax.axis_size("rest"))])


def other_core(x):
    return lax.ppermute(x, "rest", [(i, i ^ 1) for i in range(lax.axis_size("rest"))])


def other_half(x):
    return lax.ppermute(x, "hi", [(0, 1), (1, 0)])


def local(
    memory,
    last_time,
    event_time,
    edge_features,
    update_slot,
    update_serve,
    lookup_slot,
    lookup_serve,
    neighbour_gap,
    hub_node,
    hub_choice,
    time_freq,
    time_phase,
    gru_weight,
    gru_bias,
    query_weight,
    keyval_weight,
    output_weight,
):
    ev_size, hi_size, low_size, rest_size = (lax.axis_size(a) for a in BOTH)
    ev, hi, _, rest_index = (lax.axis_index(a) for a in BOTH)
    near = ev_size * low_size * rest_size
    devices = hi_size * near
    sizes = (ev_size, low_size, rest_size)
    nodes, width = memory.shape
    events = event_time.shape[0]
    slots = update_serve.shape[1]
    cap = slots // devices
    cap_lookup = lookup_serve.shape[1] // devices
    block = -(-cap_lookup // 8) * 8
    enc_width = time_freq.shape[0]
    edge_width = edge_features.shape[1]
    freq, phase = time_freq[None, :], time_phase[None, :]
    shape, sent_shape = jax.ShapeDtypeStruct, pltpu.HBM

    shared = cores_share(gru_weight)
    total, half = gru_weight.shape[0], gru_weight.shape[1] // 2
    rows = call(
        serve_kernel,
        "serve_endpoints",
        sent_shape((slots, width), BF),
        (),
        (update_serve, memory),
        (),
        fetched=(update_serve, memory),
    )
    if shared:
        late_weight = after(gru_weight, rows)
        side, column_at = rest_index // 2 % 2, rest_index % 2 * half
        first = other_ev(
            lax.dynamic_slice(late_weight, (side * SHARED, column_at), (SHARED, half))
        )
        piece = half
        core, other = rest_index % 2, 2 * (1 - ev)
        place = [2 * ev, 2 * ev + 1, other + core, other + 1 - core]
    else:
        whole = lax.all_gather(gru_weight, "ev", axis=1, tiled=True)
        piece, place = whole.shape[1], [jnp.int32(0)]
    scalars = jnp.stack([hi] + place + [rest_index // 2 % 2]).astype(jnp.int32)
    fetched = exchange(rows.reshape(devices, cap, width), BOTH).reshape(slots, width)

    lookup_row = lookup_serve
    if block != cap_lookup:
        lookup_row = jnp.pad(
            lookup_serve.reshape(devices, cap_lookup),
            ((0, 0), (0, block - cap_lookup)),
            constant_values=-1,
        ).reshape(1, devices * block)
    raw = (
        after(update_serve, rows),
        last_time[None, :],
        event_time[None, :],
        edge_features.T,
        update_slot.T,
        lookup_row,
        freq,
        phase,
    )
    rows_shape = pltpu.VMEM((near * block // LANES, LANES), F32)
    packed = cap % 16 == 0
    sent_lines = (devices, cap // 2, LANES) if packed else (slots, LANES)
    message_shape = (slots, width + LANES)
    if packed:
        message_shape = (devices, cap * width // LANES + cap // 2, LANES)
    tau, swap, sent, near_index, away_index = call(
        functools.partial(prepare_kernel, enc_width, sizes),
        "prepare",
        (
            pltpu.VMEM((slots + 16, LANES), F32),
            pltpu.VMEM((slots, slots), BF),
            pltpu.VMEM(sent_lines, BF),
            rows_shape,
            rows_shape,
        ),
        (scalars,),
        raw,
        (),
        fetched=raw,
        scratch=(pltpu.VMEM((devices * block, LANES), F32),),
    )
    if shared:
        sent = after(sent, first)
    message = call(
        partner_kernel,
        "partner_rows",
        sent_shape(message_shape, BF),
        (),
        (),
        (fetched,),
        kept=(swap, sent),
    )
    if shared:
        late_weight = after(gru_weight, rows)
        lower = other_ev(lax.dynamic_slice(late_weight, (DIRECT, column_at), (total - DIRECT, half)))
        first = after(first, message)
        second = other_x(first)
        pieces = [first, second, after(lower, second)]
        pieces += [other_core(x) for x in pieces]
    else:
        pieces = [whole]
    message = exchange(message.reshape(devices, -1, message_shape[-1]), BOTH)
    raw = (update_serve, memory, gru_bias, gru_weight)
    parts = pltpu.VMEM((3 * width // piece, nodes, piece), F32)
    new_memory, extended, near_rows = call(
        functools.partial(update_kernel, enc_width, edge_width, shared),
        "update_memory",
        (
            sent_shape((nodes, width), BF),
            sent_shape((nodes + 16, width), BF),
            sent_shape((near * block, width), BF),
        ),
        (scalars, hub_node),
        raw,
        (message.reshape(message_shape), *pieces),
        kept=(tau, near_index, away_index),
        fetched=raw,
        scratch=(
            parts,
            parts,
            pltpu.VMEM((nodes + 16, width), BF),
            pltpu.VMEM((near * block, width), BF),
        ),
        left=(0, 1, 2),
        limit=28,
    )
    other_extended = other_half(extended)
    near_looked = exchange(near_rows.reshape(near, block, width), NEAR)
    far_rows = call(
        far_kernel,
        "far_rows",
        sent_shape((near, block * width // LANES + 8, LANES), BF),
        (),
        (extended,),
        (other_extended,),
        fetched=(shape((16, width), BF),),
        flops=3 * 10**10,
    )
    far_looked = exchange(far_rows, NEAR)
    raw = (lookup_slot.T, hub_choice.T, neighbour_gap.T, freq, phase)
    routes, near_count = lookup_slot.shape[1] * events, neighbour_gap.shape[1] * events
    picked, pick_far, pick_hub, enc, own_enc = call(
        functools.partial(pick_kernel, cap_lookup, sizes[1:]),
        "pick_near",
        (
            pltpu.VMEM((routes, width), BF),
            pltpu.VMEM(lookup_slot.T.shape, F32),
            pltpu.VMEM(hub_choice.T.shape, F32),
            sent_shape((near_count, LANES), BF),
            pltpu.VMEM((8, LANES), BF),
        ),
        (scalars,),
        raw,
        (near_looked,),
        fetched=raw,
    )
    raw = (keyval_weight, enc, query_weight, output_weight)
    embedding = call(
        attend_kernel,
        "attend",
        sent_shape((events, width), BF),
        (),
        raw,
        (far_looked,),
        kept=(picked, pick_far, pick_hub, own_enc),
        fetched=raw,
    )
    return (new_memory, embedding)


def solution(mesh):
    ev_size, mem_size = mesh.devices.shape
    split = jax.sharding.Mesh(mesh.devices.reshape(ev_size, 2, 2, mem_size // 4), BOTH)
    both = P(BOTH)
    rows = P(BOTH, None)
    return jax.shard_map(
        local,
        mesh=split,
        in_specs=(
            rows,
            both,
            both,
            rows,
            rows,
            rows,
            rows,
            rows,
            rows,
            both,
            rows,
            P(),
            P(),
            P(None, "ev"),
            P(),
            P(),
            P(),
            P(),
        ),
        out_specs=(rows, rows),
        check_vma=False,
    )
```

```python
import functools
import math

import jax
import jax.numpy as jnp
from jax import lax
from jax.experimental import pallas as pl
from jax.experimental.pallas import tpu as pltpu
from jax.sharding import PartitionSpec as P

HEADS = 2
LANES = 128
SHARED = 384
DIRECT = 2 * SHARED
BF = jnp.bfloat16
F32 = jnp.float32
BOTH = ("ev", "hi", "low", "rest")
NEAR = ("ev", "rest", "low")
VMEM = pl.BlockSpec(memory_space=pltpu.VMEM)
SMEM = pl.BlockSpec(memory_space=pltpu.SMEM)
HBM = pl.BlockSpec(memory_space=pltpu.HBM)
MIB = 1024 * 1024


def dot(a, b):
    return jnp.dot(a, b, preferred_element_type=F32)


def dot_t(a, b):
    return lax.dot_general(a, b, (((1,), (1,)), ((), ())), preferred_element_type=F32)


def cosine(x):
    turns = jnp.floor(x * (0.5 / math.pi) + 0.5)
    rest = (x - turns * 6.28125) - turns * (2.0 * math.pi - 6.28125)
    square = rest * rest
    value = jnp.full_like(square, 1.0 / math.factorial(16))
    for order in range(14, -2, -2):
        sign = 1.0 if order % 4 == 0 else -1.0
        value = value * square + sign / math.factorial(order)
    return value


def sigmoid(x):
    return 0.5 * jnp.tanh(0.5 * x) + 0.5


def floor_div(x, n):
    return jnp.floor((x + 0.5) * (1.0 / n))


def columns(row):
    parts = []
    for start in range(0, row.shape[1], LANES):
        part = jnp.broadcast_to(row[:, start : start + LANES], (LANES, LANES))
        parts.append(part.T)
    return jnp.concatenate(parts, axis=0)


def one_hot(column, width):
    lane = lax.broadcasted_iota(jnp.int32, column.shape, 1).astype(F32)
    parts = [(column - start == lane).astype(F32).astype(BF) for start in range(0, width, LANES)]
    return jnp.concatenate(parts, axis=1)


def one_hot_rows(row, height):
    line = lax.broadcasted_iota(jnp.int32, (height, row.shape[1]), 0).astype(F32)
    return (line == row).astype(F32)


def lanes(row):
    return jnp.concatenate([row, jnp.zeros((1, LANES - row.shape[1]), row.dtype)], axis=1)


def fetch(pairs, sems):
    copies = [pltpu.make_async_copy(a, b, sems.at[i]) for i, (a, b) in enumerate(pairs)]
    for copy in copies:
        copy.start()
    return copies


def serve_kernel(serve_hbm, memory_hbm, rows_ref, serve, memory, sems):
    copies = fetch([(serve_hbm, serve), (memory_hbm, memory)], sems)
    copies[0].wait()
    picks = one_hot(columns(serve[...].astype(F32)), memory.shape[0])
    copies[1].wait()
    rows_ref[...] = dot(picks, memory[...]).astype(BF)


def prepare_kernel(
    enc_width,
    sizes,
    scalar_ref,
    serve_hbm,
    time_hbm,
    stamp_hbm,
    edge_hbm,
    slot_hbm,
    lookup_hbm,
    freq_hbm,
    phase_hbm,
    tau_ref,
    swap_ref,
    sent_ref,
    near_ref,
    away_ref,
    serve,
    time,
    stamp,
    edge,
    slot,
    lookup,
    freq,
    phase,
    column,
    sems,
):
    copies = fetch(
        [
            (serve_hbm, serve),
            (time_hbm, time),
            (stamp_hbm, stamp),
            (edge_hbm, edge),
            (slot_hbm, slot),
            (lookup_hbm, lookup),
            (freq_hbm, freq),
            (phase_hbm, phase),
        ],
        sems,
    )
    for copy in copies:
        copy.wait()
    column[...] = columns(lookup[...].astype(F32))
    of_half(scalar_ref[0], column, near_ref, *sizes)
    of_half(1 - scalar_ref[0], column, away_ref, *sizes)
    picks = one_hot(columns(serve[...].astype(F32)), time.shape[1]).astype(F32)
    tau = jnp.sum(picks * time[...].astype(F32), axis=1, keepdims=True)
    slots = serve.shape[1]
    tau_ref[:slots, :] = jnp.broadcast_to(tau, (slots, LANES))
    tau_ref[slots : slots + 8, :] = jnp.broadcast_to(lanes(freq[...]), (8, LANES))
    tau_ref[slots + 8 : slots + 16, :] = jnp.broadcast_to(lanes(phase[...]), (8, LANES))
    first, second = (
        one_hot_rows(slot[c : c + 1, :].astype(F32), swap_ref.shape[0]) for c in range(2)
    )
    ends = jnp.concatenate([first, second], axis=1).astype(BF)
    others = jnp.concatenate([second, first], axis=1).astype(BF)
    swap_ref[...] = dot_t(ends, others).astype(BF)
    edges = edge.shape[0]
    first_edges = LANES - enc_width
    rest = edges - first_edges
    line = lax.broadcasted_iota(jnp.int32, (LANES, edges), 0)
    entry = lax.broadcasted_iota(jnp.int32, (LANES, edges), 1)
    wanted = jnp.where(line >= enc_width, line - enc_width, line + first_edges)
    shown = (line >= enc_width) | (line < rest)
    spread = ((wanted == entry) & shown).astype(F32).astype(BF)
    extra = dot(spread, edge[...])
    stamps = stamp[...].astype(F32)
    high = floor_div(stamps, 8)
    line = lax.broadcasted_iota(jnp.int32, extra.shape, 0)
    extra = jnp.where(line == rest, high, extra)
    extra = jnp.where(line == rest + 1, stamps - 8.0 * high, extra)
    sent = dot_t((first + second).astype(BF), extra.astype(BF))
    if len(sent_ref.shape) == 3:
        sent = sent.reshape(sent_ref.shape[0], -1, LANES)
        lines = sent_ref.shape[1]
        sent = sent[:, :lines, :] + half_turn(sent[:, lines:, :])
    sent_ref[...] = sent.astype(BF)


def of_half(half, column, rows_ref, ev_size, low_size, rest_size):
    block = column.shape[0] // (ev_size * 2 * low_size * rest_size)
    parts = []
    for e in range(ev_size):
        for r in range(rest_size):
            for w in range(low_size):
                start = ((2 * e + half) * low_size + w) * rest_size + r
                parts.append(column[pl.ds(pl.multiple_of(start * block, 8), block), :])
    joined = jnp.concatenate(parts, axis=0)
    for i in range(rows_ref.shape[0]):
        rows_ref[i : i + 1, :] = joined[i * LANES : (i + 1) * LANES, :].T[:1, :]


def flat_columns(rows_ref, begin, end):
    return jnp.concatenate([columns(rows_ref[i : i + 1, :]) for i in range(begin, end)], axis=0)


def half_turn(x):
    return jnp.concatenate([x[..., LANES // 2 :], x[..., : LANES // 2]], axis=x.ndim - 1)


def partner_kernel(swap_ref, sent_ref, fetched_ref, out_ref):
    width = fetched_ref.shape[1]
    rows = dot(swap_ref[...], fetched_ref[...])
    if len(out_ref.shape) == 3:
        to_chunks(rows, out_ref)
        out_ref[:, out_ref.shape[1] - sent_ref.shape[1] :, :] = sent_ref[...]
    else:
        out_ref[:, :width] = rows.astype(BF)
        out_ref[:, width:] = sent_ref[...]


def to_chunks(rows, out_ref):
    blocks = out_ref.shape[0]
    lines = rows.shape[0] // blocks
    for c in range(rows.shape[1] // LANES):
        chunk = rows[:, c * LANES : (c + 1) * LANES].reshape(blocks, lines, LANES)
        out_ref[:, c * lines : (c + 1) * lines, :] = chunk.astype(BF)


def from_chunks(ref, lines, count):
    blocks = ref.shape[0]
    chunks = [
        ref[:, c * lines : (c + 1) * lines, :].reshape(blocks * lines, LANES) for c in range(count)
    ]
    return jnp.concatenate(chunks, axis=1)


def update_kernel(
    enc_width,
    edge_width,
    shared,
    scalar_ref,
    hub_ref,
    serve_hbm,
    memory_hbm,
    bias_hbm,
    own_weight_hbm,
    tau_ref,
    near_ref,
    away_ref,
    message_ref,
    *refs,
):
    count = 6 if shared else 1
    weight_refs, refs = refs[:count], refs[count:]
    new_hbm, extended_hbm, rows_hbm, serve, memory_ref, bias, own_weight = refs[:7]
    pre, hid, out, rows_out, sems = refs[7:]
    pairs = [(serve_hbm, serve), (memory_hbm, memory_ref), (bias_hbm, bias)]
    pairs += [(own_weight_hbm, own_weight)] if shared else []
    copies = fetch(pairs, sems)
    nodes, width = memory_ref.shape
    slots = serve.shape[1]
    lane = lax.broadcasted_iota(jnp.int32, (slots, LANES), 1)
    rest = enc_width + edge_width - LANES
    if len(message_ref.shape) == 3:
        lines = slots // message_ref.shape[0]
        chunks = width // LANES
        partner = from_chunks(message_ref, lines, chunks)
        extra = message_ref[:, chunks * lines :, :].astype(F32)
        extra = jnp.concatenate([extra, half_turn(extra)], axis=1).reshape(slots, LANES)
    else:
        partner = message_ref[:, :width]
        extra = message_ref[:, width:].astype(F32)
    stamp = extra[:, rest : rest + 1] * 8.0 + extra[:, rest + 1 : rest + 2]
    gap = stamp - tau_ref[:slots, :]
    enc = cosine(gap * tau_ref[slots : slots + 1, :] + tau_ref[slots + 8 : slots + 9, :])
    mixed = jnp.where(lane < enc_width, enc, extra).astype(BF)
    tail = jnp.where(lane < rest, extra, 0.0).astype(BF)
    messages = jnp.concatenate([partner, mixed, tail], axis=1)
    copies[0].wait()
    match = one_hot_rows(serve[...].astype(F32), nodes)
    counts = jnp.sum(match, axis=1, keepdims=True)
    summed = dot(match.astype(BF), messages)
    averaged = (summed / jnp.maximum(counts, 1.0)).astype(BF)
    copies[1].wait()
    memory = memory_ref[...]
    msg_width = 2 * width + enc_width + edge_width
    base = 2 * width + LANES
    left = jnp.concatenate([memory, averaged], axis=1)[:, :msg_width]
    hid_left = jnp.concatenate([jnp.zeros((nodes, rest), BF), memory], axis=1)
    piece = pre.shape[2]

    def whole(number, weight_ref):
        for start in range(0, weight_ref.shape[1], piece):
            cols = slice(start, start + piece)
            where = scalar_ref[number]
            pre[where] = dot(left, weight_ref[:msg_width, cols])
            hid[where] = dot(hid_left, weight_ref[base : base + rest + width, cols])
            number += 1

    if shared:
        for number, (mine, other, lower) in ((3, weight_refs[:3]), (4, weight_refs[3:])):
            where = scalar_ref[number]
            side = scalar_ref[5]
            halves = [left[:, :SHARED], left[:, SHARED:DIRECT]]
            first = jnp.where(side == 0, halves[0], halves[1])
            second = jnp.where(side == 0, halves[1], halves[0])
            pre[where] = (
                dot(first, mine[...])
                + dot(second, other[...])
                + dot(left[:, DIRECT:], lower[: msg_width - DIRECT, :])
            )
            hid[where] = dot(hid_left, lower[base - DIRECT :, :])
        copies[3].wait()
        whole(1, own_weight)
    else:
        whole(1, weight_refs[0])
    copies[2].wait()

    def third(ref, row, index):
        parts = []
        at, end = index * width, (index + 1) * width
        while at < end:
            inside = at % piece
            size = min(piece - inside, end - at)
            parts.append(ref[at // piece, :, inside : inside + size])
            at += size
        joined = parts[0] if len(parts) == 1 else jnp.concatenate(parts, axis=1)
        return joined + bias[row : row + 1, index * width : end]

    reset = sigmoid(third(pre, 0, 0) + third(hid, 1, 0))
    keep = sigmoid(third(pre, 0, 1) + third(hid, 1, 1))
    fresh = jnp.tanh(third(pre, 0, 2) + reset * third(hid, 1, 2))
    previous = memory.astype(F32)
    fresh = (1.0 - keep) * fresh + keep * previous
    new = jnp.where(counts > 0.0, fresh, previous).astype(BF)
    out[:nodes, :] = new
    line = lax.broadcasted_iota(jnp.int32, (16, nodes), 0)
    entry = lax.broadcasted_iota(jnp.int32, (16, nodes), 1)
    hub = ((entry == hub_ref[0]) & (line == 0)).astype(F32).astype(BF)
    out[nodes:, :] = dot(hub, new).astype(BF)
    for begin in range(0, away_ref.shape[0], 8):
        end = min(begin + 8, away_ref.shape[0])
        some = away_ref[begin:end, :]
        if end - begin < 8:
            some = jnp.concatenate([some, jnp.zeros((8 + begin - end, LANES), F32)], axis=0)
        out[nodes + 8 :, begin * 16 : begin * 16 + LANES] = some.astype(BF)
    sends = [
        pltpu.make_async_copy(out, extended_hbm, sems.at[0]),
        pltpu.make_async_copy(out.at[:nodes, :], new_hbm, sems.at[1]),
    ]
    for send in sends:
        send.start()
    count = near_ref.shape[0]
    for i, (begin, end) in enumerate(((0, count // 2), (count // 2, count))):
        some = slice(begin * LANES, end * LANES)
        rows_out[some, :] = dot(one_hot(flat_columns(near_ref, begin, end), nodes), new).astype(BF)
        sends.append(pltpu.make_async_copy(rows_out.at[some, :], rows_hbm.at[some, :], sems.at[2 + i]))
        sends[-1].start()
    for send in sends:
        send.wait()


def far_kernel(own_hbm, other_ref, out_ref, hub, sems):
    nodes, width = other_ref.shape[0] - 16, other_ref.shape[1]
    copies = fetch([(own_hbm.at[nodes:, :], hub)], sems)
    chunks = width // LANES
    near, lines, _ = out_ref.shape
    wanted = other_ref[nodes:, :].astype(F32)[8:, :]
    count = near * (lines - 8) // chunks // LANES
    index = [wanted[i % 8 : i % 8 + 1, i // 8 * LANES : (i // 8 + 1) * LANES] for i in range(count)]
    picks = one_hot(jnp.concatenate([columns(row) for row in index], axis=0), nodes)
    to_chunks(dot(picks, other_ref[:nodes, :]), out_ref)
    copies[0].wait()
    hubs = [other_ref[nodes : nodes + 1, :], hub[0:1, :]]
    parts = [h[:, c * LANES : (c + 1) * LANES].astype(F32) for h in hubs for c in range(chunks)]
    parts = jnp.concatenate(parts, axis=0).astype(BF)
    out_ref[:, lines - 8 :, :] = jnp.broadcast_to(parts[None], (near, 8, LANES))


def places(slot, hi, cap, low_size, rest_size):
    owner = floor_div(slot, cap)
    line = floor_div(owner, rest_size)
    rest = owner - rest_size * line
    half = floor_div(line, low_size)
    ev = floor_div(half, 2)
    relay = (ev * rest_size + rest) * low_size + line - low_size * half
    return relay, half - 2.0 * ev == hi, slot - cap * owner


def picks_of(index, width):
    return jnp.concatenate(
        [one_hot(columns(index[k : k + 1, :]), width) for k in range(index.shape[0])], axis=0
    )


def pick_kernel(
    cap,
    sizes,
    scalar_ref,
    slot_hbm,
    hub_hbm,
    gap_hbm,
    freq_hbm,
    phase_hbm,
    looked_ref,
    picked_ref,
    far_ref,
    hub_ref,
    enc_ref,
    own_ref,
    slot,
    hub,
    gaps,
    freq,
    phase,
    sems,
):
    copies = fetch(
        [(slot_hbm, slot), (hub_hbm, hub), (gap_hbm, gaps), (freq_hbm, freq), (phase_hbm, phase)],
        sems,
    )
    for copy in copies:
        copy.wait()
    owners, block, width = looked_ref.shape
    hi = scalar_ref[0].astype(F32)
    relay, near, place = places(slot[...].astype(F32), hi, cap, *sizes)
    index = jnp.where(near, relay * block + place, -1.0)
    looked = looked_ref[...].reshape(owners * block, width)
    events = gaps.shape[1]
    picks = [one_hot(columns(index[k : k + 1, :]), owners * block) for k in range(slot.shape[0])]
    picked_ref[...] = dot(jnp.concatenate(picks, axis=0), looked).astype(BF)
    far_ref[...] = jnp.where(near, -1.0, relay * block + place)
    relay, near, place = places(hub[...].astype(F32), hi, 1, *sizes)
    hub_ref[...] = relay * 8.0 + jnp.where(near, 4.0, 0.0)
    freq_row, phase_row = lanes(freq[...]), lanes(phase[...])
    for k in range(gaps.shape[0]):
        angle = columns(gaps[k : k + 1, :].astype(F32)) * freq_row + phase_row
        enc_ref[k * events : (k + 1) * events, :] = cosine(angle).astype(BF)
    own_ref[...] = jnp.broadcast_to(cosine(phase_row), (8, LANES)).astype(BF)


def attend_kernel(
    keyval_hbm,
    enc_hbm,
    query_hbm,
    output_hbm,
    picked_ref,
    far_ref,
    hub_ref,
    own_enc_ref,
    looked_ref,
    out_ref,
    keyval_ref,
    enc_ref,
    query_ref,
    output_ref,
    sems,
):
    copies = fetch(
        [
            (keyval_hbm, keyval_ref),
            (enc_hbm, enc_ref),
            (query_hbm, query_ref),
            (output_hbm, output_ref),
        ],
        sems,
    )
    events, width = out_ref.shape
    chunks = width // LANES
    owners = looked_ref.shape[0]
    block = (looked_ref.shape[1] - 8) // chunks
    near = enc_ref.shape[0] // events
    att = query_ref.shape[1]
    head = att // HEADS
    looked = from_chunks(looked_ref, block, chunks)
    hub_lines = looked_ref[:, chunks * block :, :].astype(F32).reshape(owners * 8, LANES)
    hub_rows = [hub_lines] + [
        jnp.concatenate([hub_lines[c:], hub_lines[:c]], axis=0) for c in range(1, chunks)
    ]
    hub_rows = jnp.concatenate(hub_rows, axis=1).astype(BF)
    hub_near = dot(picks_of(hub_ref[...], owners * 8), hub_rows).astype(BF)
    picks = picks_of(far_ref[...], owners * block)
    rows = dot(picks, looked).astype(BF) + picked_ref[...]
    own = rows[:events]
    near_rows = jnp.concatenate([rows[events:], hub_near], axis=0)
    copies[0].wait()
    copies[1].wait()
    key_width = keyval_ref.shape[0]
    key_input = jnp.concatenate([near_rows, enc_ref[...]], axis=1)[:, :key_width]
    keyval = dot(key_input, keyval_ref[...]).astype(BF).astype(F32)
    copies[2].wait()
    own_enc = jnp.broadcast_to(own_enc_ref[0:1, :], (events, LANES))
    query_input = jnp.concatenate([own, own_enc], axis=1)[:, :key_width]
    query = dot(query_input, query_ref[...]).astype(BF).astype(F32)
    mixed = []
    for h in range(HEADS):
        cols = slice(h * head, (h + 1) * head)
        vals = slice(att + h * head, att + (h + 1) * head)
        slabs = [slice(k * events, (k + 1) * events) for k in range(near)]
        scores = [
            jnp.sum(query[:, cols] * keyval[s, cols], axis=1, keepdims=True) * head**-0.5
            for s in slabs
        ]
        top = functools.reduce(jnp.maximum, scores)
        expo = [jnp.exp(s - top) for s in scores]
        total = functools.reduce(jnp.add, expo)
        prob = [(e / total).astype(BF).astype(F32) for e in expo]
        mixed.append(sum(p * keyval[s, vals] for p, s in zip(prob, slabs)))
    joined = jnp.concatenate([m.astype(BF) for m in mixed] + [own], axis=1)
    copies[3].wait()
    out_ref[...] = dot(joined, output_ref[...]).astype(BF)


def exchange(x, axes):
    return lax.all_to_all(x, axes, split_axis=0, concat_axis=0, tiled=True)


def after(x, *earlier):
    return lax.optimization_barrier((x, *earlier))[0]


def call(kernel, name, out_shape, smem, hbm, vmem, fetched=(), scratch=(), left=(), kept=(), limit=20, extra_sems=0, flops=0):
    many = isinstance(out_shape, tuple)
    specs = tuple(HBM if x in left else VMEM for x in range(len(out_shape))) if many else VMEM
    copies = [pltpu.VMEM(x.shape, x.dtype) for x in fetched]
    sems = [pltpu.SemaphoreType.DMA((len(fetched) + extra_sems,))] if fetched else []
    return pl.pallas_call(
        kernel,
        out_shape=out_shape,
        in_specs=[SMEM] * len(smem) + [HBM] * len(hbm) + [VMEM] * (len(kept) + len(vmem)),
        out_specs=specs,
        scratch_shapes=copies + list(scratch) + sems,
        compiler_params=pltpu.CompilerParams(vmem_limit_bytes=limit * MIB),
        name=name,
        cost_estimate=pl.CostEstimate(flops=flops, bytes_accessed=0, transcendentals=0) if flops else None,
    )(*smem, *[pltpu.with_memory_space_constraint(x, pltpu.HBM) for x in hbm], *[pltpu.with_memory_space_constraint(x, pltpu.VMEM) for x in kept], *vmem)


def cores_share(gru_weight):
    half = gru_weight.shape[1] // 2
    return lax.axis_size("ev") == 2 and lax.axis_size("rest") % 4 == 0 and half % LANES == 0


def other_ev(x):
    return lax.ppermute(x, "ev", [(0, 1), (1, 0)])


def other_x(x):
    return lax.ppermute(x, "rest", [(i, i ^ 2) for i in range(lax.axis_size("rest"))])


def other_core(x):
    return lax.ppermute(x, "rest", [(i, i ^ 1) for i in range(lax.axis_size("rest"))])


def other_half(x):
    return lax.ppermute(x, "hi", [(0, 1), (1, 0)])


def local(
    memory,
    last_time,
    event_time,
    edge_features,
    update_slot,
    update_serve,
    lookup_slot,
    lookup_serve,
    neighbour_gap,
    hub_node,
    hub_choice,
    time_freq,
    time_phase,
    gru_weight,
    gru_bias,
    query_weight,
    keyval_weight,
    output_weight,
):
    ev_size, hi_size, low_size, rest_size = (lax.axis_size(a) for a in BOTH)
    ev, hi, _, rest_index = (lax.axis_index(a) for a in BOTH)
    near = ev_size * low_size * rest_size
    devices = hi_size * near
    sizes = (ev_size, low_size, rest_size)
    nodes, width = memory.shape
    events = event_time.shape[0]
    slots = update_serve.shape[1]
    cap = slots // devices
    cap_lookup = lookup_serve.shape[1] // devices
    block = -(-cap_lookup // 8) * 8
    enc_width = time_freq.shape[0]
    edge_width = edge_features.shape[1]
    freq, phase = time_freq[None, :], time_phase[None, :]
    shape, sent_shape = jax.ShapeDtypeStruct, pltpu.HBM

    shared = cores_share(gru_weight)
    total, half = gru_weight.shape[0], gru_weight.shape[1] // 2
    rows = call(
        serve_kernel,
        "serve_endpoints",
        sent_shape((slots, width), BF),
        (),
        (update_serve, memory),
        (),
        fetched=(update_serve, memory),
    )
    if shared:
        late_weight = after(gru_weight, rows)
        side, column_at = rest_index // 2 % 2, rest_index % 2 * half
        first = other_ev(
            lax.dynamic_slice(late_weight, (side * SHARED, column_at), (SHARED, half))
        )
        piece = half
        core, other = rest_index % 2, 2 * (1 - ev)
        place = [2 * ev, 2 * ev + 1, other + core, other + 1 - core]
    else:
        whole = lax.all_gather(gru_weight, "ev", axis=1, tiled=True)
        piece, place = whole.shape[1], [jnp.int32(0)]
    scalars = jnp.stack([hi] + place + [rest_index // 2 % 2]).astype(jnp.int32)
    fetched = exchange(rows.reshape(devices, cap, width), BOTH).reshape(slots, width)

    lookup_row = lookup_serve
    if block != cap_lookup:
        lookup_row = jnp.pad(
            lookup_serve.reshape(devices, cap_lookup),
            ((0, 0), (0, block - cap_lookup)),
            constant_values=-1,
        ).reshape(1, devices * block)
    raw = (
        after(update_serve, rows),
        last_time[None, :],
        event_time[None, :],
        edge_features.T,
        update_slot.T,
        lookup_row,
        freq,
        phase,
    )
    rows_shape = pltpu.VMEM((near * block // LANES, LANES), F32)
    packed = cap % 16 == 0
    sent_lines = (devices, cap // 2, LANES) if packed else (slots, LANES)
    message_shape = (slots, width + LANES)
    if packed:
        message_shape = (devices, cap * width // LANES + cap // 2, LANES)
    tau, swap, sent, near_index, away_index = call(
        functools.partial(prepare_kernel, enc_width, sizes),
        "prepare",
        (
            pltpu.VMEM((slots + 16, LANES), F32),
            pltpu.VMEM((slots, slots), BF),
            pltpu.VMEM(sent_lines, BF),
            rows_shape,
            rows_shape,
        ),
        (scalars,),
        raw,
        (),
        fetched=raw,
        scratch=(pltpu.VMEM((devices * block, LANES), F32),),
    )
    if shared:
        sent = after(sent, first)
    message = call(
        partner_kernel,
        "partner_rows",
        sent_shape(message_shape, BF),
        (),
        (),
        (fetched,),
        kept=(swap, sent),
    )
    if shared:
        late_weight = after(gru_weight, rows)
        lower = other_ev(lax.dynamic_slice(late_weight, (DIRECT, column_at), (total - DIRECT, half)))
        first = after(first, message)
        second = other_x(first)
        pieces = [first, second, after(lower, second)]
        pieces += [other_core(x) for x in pieces]
    else:
        pieces = [whole]
    message = exchange(message.reshape(devices, -1, message_shape[-1]), BOTH)
    raw = (update_serve, memory, gru_bias, gru_weight)
    parts = pltpu.VMEM((3 * width // piece, nodes, piece), F32)
    new_memory, extended, near_rows = call(
        functools.partial(update_kernel, enc_width, edge_width, shared),
        "update_memory",
        (
            sent_shape((nodes, width), BF),
            sent_shape((nodes + 16, width), BF),
            sent_shape((near * block, width), BF),
        ),
        (scalars, hub_node),
        raw,
        (message.reshape(message_shape), *pieces),
        kept=(tau, near_index, away_index),
        fetched=raw,
        scratch=(
            parts,
            parts,
            pltpu.VMEM((nodes + 16, width), BF),
            pltpu.VMEM((near * block, width), BF),
        ),
        left=(0, 1, 2),
        limit=28,
    )
    other_extended = other_half(extended)
    near_looked = exchange(near_rows.reshape(near, block, width), NEAR)
    far_rows = call(
        far_kernel,
        "far_rows",
        sent_shape((near, block * width // LANES + 8, LANES), BF),
        (),
        (extended,),
        (other_extended,),
        fetched=(shape((16, width), BF),),
        flops=3 * 10**10,
    )
    far_looked = exchange(far_rows, NEAR)
    raw = (lookup_slot.T, hub_choice.T, neighbour_gap.T, freq, phase)
    routes, near_count = lookup_slot.shape[1] * events, neighbour_gap.shape[1] * events
    picked, pick_far, pick_hub, enc, own_enc = call(
        functools.partial(pick_kernel, cap_lookup, sizes[1:]),
        "pick_near",
        (
            pltpu.VMEM((routes, width), BF),
            pltpu.VMEM(lookup_slot.T.shape, F32),
            pltpu.VMEM(hub_choice.T.shape, F32),
            sent_shape((near_count, LANES), BF),
            pltpu.VMEM((8, LANES), BF),
        ),
        (scalars,),
        raw,
        (near_looked,),
        fetched=raw,
    )
    raw = (keyval_weight, enc, query_weight, output_weight)
    embedding = call(
        attend_kernel,
        "attend",
        sent_shape((events, width), BF),
        (),
        raw,
        (far_looked,),
        kept=(picked, pick_far, pick_hub, own_enc),
        fetched=raw,
    )
    return (new_memory, embedding)


def solution(mesh):
    ev_size, mem_size = mesh.devices.shape
    split = jax.sharding.Mesh(mesh.devices.reshape(ev_size, 2, 2, mem_size // 4), BOTH)
    both = P(BOTH)
    rows = P(BOTH, None)
    return jax.shard_map(
        local,
        mesh=split,
        in_specs=(
            rows,
            both,
            both,
            rows,
            rows,
            rows,
            rows,
            rows,
            rows,
            both,
            rows,
            P(),
            P(),
            P(None, "ev"),
            P(),
            P(),
            P(),
            P(),
        ),
        out_specs=(rows, rows),
        check_vma=False,
    )
```

```python
import functools
import math

import jax
import jax.numpy as jnp
from jax import lax
from jax.experimental import pallas as pl
from jax.experimental.pallas import tpu as pltpu
from jax.sharding import PartitionSpec as P

HEADS = 2
LANES = 128
SHARED = 384
DIRECT = 2 * SHARED
BF = jnp.bfloat16
F32 = jnp.float32
BOTH = ("ev", "hi", "low", "rest")
NEAR = ("ev", "rest", "low")
VMEM = pl.BlockSpec(memory_space=pltpu.VMEM)
SMEM = pl.BlockSpec(memory_space=pltpu.SMEM)
HBM = pl.BlockSpec(memory_space=pltpu.HBM)
MIB = 1024 * 1024


def dot(a, b):
    return jnp.dot(a, b, preferred_element_type=F32)


def dot_t(a, b):
    return lax.dot_general(a, b, (((1,), (1,)), ((), ())), preferred_element_type=F32)


def cosine(x):
    turns = jnp.floor(x * (0.5 / math.pi) + 0.5)
    rest = (x - turns * 6.28125) - turns * (2.0 * math.pi - 6.28125)
    square = rest * rest
    value = jnp.full_like(square, 1.0 / math.factorial(16))
    for order in range(14, -2, -2):
        sign = 1.0 if order % 4 == 0 else -1.0
        value = value * square + sign / math.factorial(order)
    return value


def sigmoid(x):
    return 0.5 * jnp.tanh(0.5 * x) + 0.5


def floor_div(x, n):
    return jnp.floor((x + 0.5) * (1.0 / n))


def columns(row):
    parts = []
    for start in range(0, row.shape[1], LANES):
        part = jnp.broadcast_to(row[:, start : start + LANES], (LANES, LANES))
        parts.append(part.T)
    return jnp.concatenate(parts, axis=0)


def one_hot(column, width):
    lane = lax.broadcasted_iota(jnp.int32, column.shape, 1).astype(F32)
    parts = [(column - start == lane).astype(F32).astype(BF) for start in range(0, width, LANES)]
    return jnp.concatenate(parts, axis=1)


def one_hot_rows(row, height):
    line = lax.broadcasted_iota(jnp.int32, (height, row.shape[1]), 0).astype(F32)
    return (line == row).astype(F32)


def lanes(row):
    return jnp.concatenate([row, jnp.zeros((1, LANES - row.shape[1]), row.dtype)], axis=1)


def fetch(pairs, sems):
    copies = [pltpu.make_async_copy(a, b, sems.at[i]) for i, (a, b) in enumerate(pairs)]
    for copy in copies:
        copy.start()
    return copies


def serve_kernel(serve_hbm, memory_hbm, rows_hbm, serve, memory, out, sems):
    copies = fetch([(serve_hbm, serve), (memory_hbm, memory)], sems)
    copies[0].wait()
    picks = one_hot(columns(serve[...].astype(F32)), memory.shape[0])
    copies[1].wait()
    half = out.shape[0] // 2
    sends = []
    for n in range(2):
        some = slice(n * half, (n + 1) * half)
        out[some, :] = dot(picks[some, :], memory[...]).astype(BF)
        sends.append(pltpu.make_async_copy(out.at[some, :], rows_hbm.at[some, :], sems.at[2 + n]))
        sends[n].start()
    for send in sends:
        send.wait()


def prepare_kernel(
    enc_width,
    sizes,
    scalar_ref,
    serve_hbm,
    time_hbm,
    stamp_hbm,
    edge_hbm,
    slot_hbm,
    lookup_hbm,
    freq_hbm,
    phase_hbm,
    tau_ref,
    swap_ref,
    sent_ref,
    near_ref,
    away_ref,
    serve,
    time,
    stamp,
    edge,
    slot,
    lookup,
    freq,
    phase,
    column,
    sems,
):
    copies = fetch(
        [
            (serve_hbm, serve),
            (time_hbm, time),
            (stamp_hbm, stamp),
            (edge_hbm, edge),
            (slot_hbm, slot),
            (lookup_hbm, lookup),
            (freq_hbm, freq),
            (phase_hbm, phase),
        ],
        sems,
    )
    for copy in copies:
        copy.wait()
    column[...] = columns(lookup[...].astype(F32))
    of_half(scalar_ref[0], column, near_ref, *sizes)
    of_half(1 - scalar_ref[0], column, away_ref, *sizes)
    picks = one_hot(columns(serve[...].astype(F32)), time.shape[1]).astype(F32)
    tau = jnp.sum(picks * time[...].astype(F32), axis=1, keepdims=True)
    slots = serve.shape[1]
    tau_ref[:slots, :] = jnp.broadcast_to(tau, (slots, LANES))
    tau_ref[slots : slots + 8, :] = jnp.broadcast_to(lanes(freq[...]), (8, LANES))
    tau_ref[slots + 8 : slots + 16, :] = jnp.broadcast_to(lanes(phase[...]), (8, LANES))
    first, second = (
        one_hot_rows(slot[c : c + 1, :].astype(F32), swap_ref.shape[0]) for c in range(2)
    )
    ends = jnp.concatenate([first, second], axis=1).astype(BF)
    others = jnp.concatenate([second, first], axis=1).astype(BF)
    swap_ref[...] = dot_t(ends, others).astype(BF)
    edges = edge.shape[0]
    first_edges = LANES - enc_width
    rest = edges - first_edges
    line = lax.broadcasted_iota(jnp.int32, (LANES, edges), 0)
    entry = lax.broadcasted_iota(jnp.int32, (LANES, edges), 1)
    wanted = jnp.where(line >= enc_width, line - enc_width, line + first_edges)
    shown = (line >= enc_width) | (line < rest)
    spread = ((wanted == entry) & shown).astype(F32).astype(BF)
    extra = dot(spread, edge[...])
    stamps = stamp[...].astype(F32)
    high = floor_div(stamps, 8)
    line = lax.broadcasted_iota(jnp.int32, extra.shape, 0)
    extra = jnp.where(line == rest, high, extra)
    extra = jnp.where(line == rest + 1, stamps - 8.0 * high, extra)
    sent = dot_t((first + second).astype(BF), extra.astype(BF))
    if len(sent_ref.shape) == 3:
        sent = sent.reshape(sent_ref.shape[0], -1, LANES)
        lines = sent_ref.shape[1]
        sent = sent[:, :lines, :] + half_turn(sent[:, lines:, :])
    sent_ref[...] = sent.astype(BF)


def of_half(half, column, rows_ref, ev_size, low_size, rest_size):
    block = column.shape[0] // (ev_size * 2 * low_size * rest_size)
    parts = []
    for e in range(ev_size):
        for r in range(rest_size):
            for w in range(low_size):
                start = ((2 * e + half) * low_size + w) * rest_size + r
                parts.append(column[pl.ds(pl.multiple_of(start * block, 8), block), :])
    joined = jnp.concatenate(parts, axis=0)
    for i in range(rows_ref.shape[0]):
        rows_ref[i : i + 1, :] = joined[i * LANES : (i + 1) * LANES, :].T[:1, :]


def flat_columns(rows_ref, begin, end):
    return jnp.concatenate([columns(rows_ref[i : i + 1, :]) for i in range(begin, end)], axis=0)


def half_turn(x):
    return jnp.concatenate([x[..., LANES // 2 :], x[..., : LANES // 2]], axis=x.ndim - 1)


def partner_kernel(swap_ref, sent_ref, fetched_ref, out_ref):
    width = fetched_ref.shape[1]
    rows = dot(swap_ref[...], fetched_ref[...])
    if len(out_ref.shape) == 3:
        to_chunks(rows, out_ref)
        out_ref[:, out_ref.shape[1] - sent_ref.shape[1] :, :] = sent_ref[...]
    else:
        out_ref[:, :width] = rows.astype(BF)
        out_ref[:, width:] = sent_ref[...]


def to_chunks(rows, out_ref):
    blocks = out_ref.shape[0]
    lines = rows.shape[0] // blocks
    for c in range(rows.shape[1] // LANES):
        chunk = rows[:, c * LANES : (c + 1) * LANES].reshape(blocks, lines, LANES)
        out_ref[:, c * lines : (c + 1) * lines, :] = chunk.astype(BF)


def from_chunks(ref, lines, count):
    blocks = ref.shape[0]
    chunks = [
        ref[:, c * lines : (c + 1) * lines, :].reshape(blocks * lines, LANES) for c in range(count)
    ]
    return jnp.concatenate(chunks, axis=1)


def update_kernel(
    enc_width,
    edge_width,
    shared,
    scalar_ref,
    hub_ref,
    serve_hbm,
    memory_hbm,
    bias_hbm,
    own_weight_hbm,
    tau_ref,
    near_ref,
    away_ref,
    message_ref,
    *refs,
):
    count = 6 if shared else 1
    weight_refs, refs = refs[:count], refs[count:]
    new_hbm, extended_hbm, rows_hbm, serve, memory_ref, bias, own_weight = refs[:7]
    pre, hid, out, rows_out, sems = refs[7:]
    pairs = [(serve_hbm, serve), (memory_hbm, memory_ref), (bias_hbm, bias)]
    pairs += [(own_weight_hbm, own_weight)] if shared else []
    copies = fetch(pairs, sems)
    nodes, width = memory_ref.shape
    slots = serve.shape[1]
    lane = lax.broadcasted_iota(jnp.int32, (slots, LANES), 1)
    rest = enc_width + edge_width - LANES
    if len(message_ref.shape) == 3:
        lines = slots // message_ref.shape[0]
        chunks = width // LANES
        partner = from_chunks(message_ref, lines, chunks)
        extra = message_ref[:, chunks * lines :, :].astype(F32)
        extra = jnp.concatenate([extra, half_turn(extra)], axis=1).reshape(slots, LANES)
    else:
        partner = message_ref[:, :width]
        extra = message_ref[:, width:].astype(F32)
    stamp = extra[:, rest : rest + 1] * 8.0 + extra[:, rest + 1 : rest + 2]
    gap = stamp - tau_ref[:slots, :]
    enc = cosine(gap * tau_ref[slots : slots + 1, :] + tau_ref[slots + 8 : slots + 9, :])
    mixed = jnp.where(lane < enc_width, enc, extra).astype(BF)
    tail = jnp.where(lane < rest, extra, 0.0).astype(BF)
    messages = jnp.concatenate([partner, mixed, tail], axis=1)
    copies[0].wait()
    match = one_hot_rows(serve[...].astype(F32), nodes)
    counts = jnp.sum(match, axis=1, keepdims=True)
    summed = dot(match.astype(BF), messages)
    averaged = (summed / jnp.maximum(counts, 1.0)).astype(BF)
    copies[1].wait()
    memory = memory_ref[...]
    msg_width = 2 * width + enc_width + edge_width
    base = 2 * width + LANES
    left = jnp.concatenate([memory, averaged], axis=1)[:, :msg_width]
    hid_left = jnp.concatenate([jnp.zeros((nodes, rest), BF), memory], axis=1)
    piece = pre.shape[2]

    def whole(number, weight_ref):
        for start in range(0, weight_ref.shape[1], piece):
            cols = slice(start, start + piece)
            where = scalar_ref[number]
            pre[where] = dot(left, weight_ref[:msg_width, cols])
            hid[where] = dot(hid_left, weight_ref[base : base + rest + width, cols])
            number += 1

    if shared:
        for number, (mine, other, lower) in ((3, weight_refs[:3]), (4, weight_refs[3:])):
            where = scalar_ref[number]
            side = scalar_ref[5]
            halves = [left[:, :SHARED], left[:, SHARED:DIRECT]]
            first = jnp.where(side == 0, halves[0], halves[1])
            second = jnp.where(side == 0, halves[1], halves[0])
            pre[where] = (
                dot(first, mine[...])
                + dot(second, other[...])
                + dot(left[:, DIRECT:], lower[: msg_width - DIRECT, :])
            )
            hid[where] = dot(hid_left, lower[base - DIRECT :, :])
        copies[3].wait()
        whole(1, own_weight)
    else:
        whole(1, weight_refs[0])
    copies[2].wait()

    def third(ref, row, index):
        parts = []
        at, end = index * width, (index + 1) * width
        while at < end:
            inside = at % piece
            size = min(piece - inside, end - at)
            parts.append(ref[at // piece, :, inside : inside + size])
            at += size
        joined = parts[0] if len(parts) == 1 else jnp.concatenate(parts, axis=1)
        return joined + bias[row : row + 1, index * width : end]

    reset = sigmoid(third(pre, 0, 0) + third(hid, 1, 0))
    keep = sigmoid(third(pre, 0, 1) + third(hid, 1, 1))
    fresh = jnp.tanh(third(pre, 0, 2) + reset * third(hid, 1, 2))
    previous = memory.astype(F32)
    fresh = (1.0 - keep) * fresh + keep * previous
    new = jnp.where(counts > 0.0, fresh, previous).astype(BF)
    out[:nodes, :] = new
    line = lax.broadcasted_iota(jnp.int32, (16, nodes), 0)
    entry = lax.broadcasted_iota(jnp.int32, (16, nodes), 1)
    hub = ((entry == hub_ref[0]) & (line == 0)).astype(F32).astype(BF)
    out[nodes:, :] = dot(hub, new).astype(BF)
    for begin in range(0, away_ref.shape[0], 8):
        end = min(begin + 8, away_ref.shape[0])
        some = away_ref[begin:end, :]
        if end - begin < 8:
            some = jnp.concatenate([some, jnp.zeros((8 + begin - end, LANES), F32)], axis=0)
        out[nodes + 8 :, begin * 16 : begin * 16 + LANES] = some.astype(BF)
    sends = [
        pltpu.make_async_copy(out, extended_hbm, sems.at[0]),
        pltpu.make_async_copy(out.at[:nodes, :], new_hbm, sems.at[1]),
    ]
    for send in sends:
        send.start()
    count = near_ref.shape[0]
    for i, (begin, end) in enumerate(((0, count // 2), (count // 2, count))):
        some = slice(begin * LANES, end * LANES)
        rows_out[some, :] = dot(one_hot(flat_columns(near_ref, begin, end), nodes), new).astype(BF)
        sends.append(pltpu.make_async_copy(rows_out.at[some, :], rows_hbm.at[some, :], sems.at[2 + i]))
        sends[-1].start()
    for send in sends:
        send.wait()


def far_kernel(own_hbm, other_ref, out_ref, hub, sems):
    nodes, width = other_ref.shape[0] - 16, other_ref.shape[1]
    copies = fetch([(own_hbm.at[nodes:, :], hub)], sems)
    chunks = width // LANES
    near, lines, _ = out_ref.shape
    wanted = other_ref[nodes:, :].astype(F32)[8:, :]
    count = near * (lines - 8) // chunks // LANES
    index = [wanted[i % 8 : i % 8 + 1, i // 8 * LANES : (i // 8 + 1) * LANES] for i in range(count)]
    picks = one_hot(jnp.concatenate([columns(row) for row in index], axis=0), nodes)
    to_chunks(dot(picks, other_ref[:nodes, :]), out_ref)
    copies[0].wait()
    hubs = [other_ref[nodes : nodes + 1, :], hub[0:1, :]]
    parts = [h[:, c * LANES : (c + 1) * LANES].astype(F32) for h in hubs for c in range(chunks)]
    parts = jnp.concatenate(parts, axis=0).astype(BF)
    out_ref[:, lines - 8 :, :] = jnp.broadcast_to(parts[None], (near, 8, LANES))


def places(slot, hi, cap, low_size, rest_size):
    owner = floor_div(slot, cap)
    line = floor_div(owner, rest_size)
    rest = owner - rest_size * line
    half = floor_div(line, low_size)
    ev = floor_div(half, 2)
    relay = (ev * rest_size + rest) * low_size + line - low_size * half
    return relay, half - 2.0 * ev == hi, slot - cap * owner


def picks_of(index, width):
    return jnp.concatenate(
        [one_hot(columns(index[k : k + 1, :]), width) for k in range(index.shape[0])], axis=0
    )


def pick_kernel(
    cap,
    sizes,
    scalar_ref,
    slot_hbm,
    hub_hbm,
    gap_hbm,
    freq_hbm,
    phase_hbm,
    looked_ref,
    picked_ref,
    far_ref,
    hub_ref,
    enc_ref,
    own_ref,
    slot,
    hub,
    gaps,
    freq,
    phase,
    sems,
):
    copies = fetch(
        [(slot_hbm, slot), (hub_hbm, hub), (gap_hbm, gaps), (freq_hbm, freq), (phase_hbm, phase)],
        sems,
    )
    for copy in copies:
        copy.wait()
    owners, block, width = looked_ref.shape
    hi = scalar_ref[0].astype(F32)
    relay, near, place = places(slot[...].astype(F32), hi, cap, *sizes)
    index = jnp.where(near, relay * block + place, -1.0)
    looked = looked_ref[...].reshape(owners * block, width)
    events = gaps.shape[1]
    picks = [one_hot(columns(index[k : k + 1, :]), owners * block) for k in range(slot.shape[0])]
    picked_ref[...] = dot(jnp.concatenate(picks, axis=0), looked).astype(BF)
    far_ref[...] = jnp.where(near, -1.0, relay * block + place)
    relay, near, place = places(hub[...].astype(F32), hi, 1, *sizes)
    hub_ref[...] = relay * 8.0 + jnp.where(near, 4.0, 0.0)
    freq_row, phase_row = lanes(freq[...]), lanes(phase[...])
    for k in range(gaps.shape[0]):
        angle = columns(gaps[k : k + 1, :].astype(F32)) * freq_row + phase_row
        enc_ref[k * events : (k + 1) * events, :] = cosine(angle).astype(BF)
    own_ref[...] = jnp.broadcast_to(cosine(phase_row), (8, LANES)).astype(BF)


def attend_kernel(
    keyval_hbm,
    enc_hbm,
    query_hbm,
    output_hbm,
    picked_ref,
    far_ref,
    hub_ref,
    own_enc_ref,
    looked_ref,
    out_ref,
    keyval_ref,
    enc_ref,
    query_ref,
    output_ref,
    sems,
):
    copies = fetch(
        [
            (keyval_hbm, keyval_ref),
            (enc_hbm, enc_ref),
            (query_hbm, query_ref),
            (output_hbm, output_ref),
        ],
        sems,
    )
    events, width = out_ref.shape
    chunks = width // LANES
    owners = looked_ref.shape[0]
    block = (looked_ref.shape[1] - 8) // chunks
    near = enc_ref.shape[0] // events
    att = query_ref.shape[1]
    head = att // HEADS
    looked = from_chunks(looked_ref, block, chunks)
    hub_lines = looked_ref[:, chunks * block :, :].astype(F32).reshape(owners * 8, LANES)
    hub_rows = [hub_lines] + [
        jnp.concatenate([hub_lines[c:], hub_lines[:c]], axis=0) for c in range(1, chunks)
    ]
    hub_rows = jnp.concatenate(hub_rows, axis=1).astype(BF)
    hub_near = dot(picks_of(hub_ref[...], owners * 8), hub_rows).astype(BF)
    picks = picks_of(far_ref[...], owners * block)
    rows = dot(picks, looked).astype(BF) + picked_ref[...]
    own = rows[:events]
    near_rows = jnp.concatenate([rows[events:], hub_near], axis=0)
    copies[0].wait()
    copies[1].wait()
    key_width = keyval_ref.shape[0]
    key_input = jnp.concatenate([near_rows, enc_ref[...]], axis=1)[:, :key_width]
    keyval = dot(key_input, keyval_ref[...]).astype(BF).astype(F32)
    copies[2].wait()
    own_enc = jnp.broadcast_to(own_enc_ref[0:1, :], (events, LANES))
    query_input = jnp.concatenate([own, own_enc], axis=1)[:, :key_width]
    query = dot(query_input, query_ref[...]).astype(BF).astype(F32)
    mixed = []
    for h in range(HEADS):
        cols = slice(h * head, (h + 1) * head)
        vals = slice(att + h * head, att + (h + 1) * head)
        slabs = [slice(k * events, (k + 1) * events) for k in range(near)]
        scores = [
            jnp.sum(query[:, cols] * keyval[s, cols], axis=1, keepdims=True) * head**-0.5
            for s in slabs
        ]
        top = functools.reduce(jnp.maximum, scores)
        expo = [jnp.exp(s - top) for s in scores]
        total = functools.reduce(jnp.add, expo)
        prob = [(e / total).astype(BF).astype(F32) for e in expo]
        mixed.append(sum(p * keyval[s, vals] for p, s in zip(prob, slabs)))
    joined = jnp.concatenate([m.astype(BF) for m in mixed] + [own], axis=1)
    copies[3].wait()
    out_ref[...] = dot(joined, output_ref[...]).astype(BF)


def exchange(x, axes):
    return lax.all_to_all(x, axes, split_axis=0, concat_axis=0, tiled=True)


def after(x, *earlier):
    return lax.optimization_barrier((x, *earlier))[0]


def call(kernel, name, out_shape, smem, hbm, vmem, fetched=(), scratch=(), left=(), kept=(), limit=20, extra_sems=0, flops=0):
    many = isinstance(out_shape, tuple)
    specs = tuple(HBM if x in left else VMEM for x in range(len(out_shape))) if many else VMEM
    copies = [pltpu.VMEM(x.shape, x.dtype) for x in fetched]
    sems = [pltpu.SemaphoreType.DMA((len(fetched) + extra_sems,))] if fetched else []
    return pl.pallas_call(
        kernel,
        out_shape=out_shape,
        in_specs=[SMEM] * len(smem) + [HBM] * len(hbm) + [VMEM] * (len(kept) + len(vmem)),
        out_specs=specs,
        scratch_shapes=copies + list(scratch) + sems,
        compiler_params=pltpu.CompilerParams(vmem_limit_bytes=limit * MIB),
        name=name,
        cost_estimate=pl.CostEstimate(flops=flops, bytes_accessed=0, transcendentals=0) if flops else None,
    )(*smem, *[pltpu.with_memory_space_constraint(x, pltpu.HBM) for x in hbm], *[pltpu.with_memory_space_constraint(x, pltpu.VMEM) for x in kept], *vmem)


def cores_share(gru_weight):
    half = gru_weight.shape[1] // 2
    return lax.axis_size("ev") == 2 and lax.axis_size("rest") % 4 == 0 and half % LANES == 0


def other_ev(x):
    return lax.ppermute(x, "ev", [(0, 1), (1, 0)])


def other_x(x):
    return lax.ppermute(x, "rest", [(i, i ^ 2) for i in range(lax.axis_size("rest"))])


def other_core(x):
    return lax.ppermute(x, "rest", [(i, i ^ 1) for i in range(lax.axis_size("rest"))])


def other_half(x):
    return lax.ppermute(x, "hi", [(0, 1), (1, 0)])


def local(
    memory,
    last_time,
    event_time,
    edge_features,
    update_slot,
    update_serve,
    lookup_slot,
    lookup_serve,
    neighbour_gap,
    hub_node,
    hub_choice,
    time_freq,
    time_phase,
    gru_weight,
    gru_bias,
    query_weight,
    keyval_weight,
    output_weight,
):
    ev_size, hi_size, low_size, rest_size = (lax.axis_size(a) for a in BOTH)
    ev, hi, _, rest_index = (lax.axis_index(a) for a in BOTH)
    near = ev_size * low_size * rest_size
    devices = hi_size * near
    sizes = (ev_size, low_size, rest_size)
    nodes, width = memory.shape
    events = event_time.shape[0]
    slots = update_serve.shape[1]
    cap = slots // devices
    cap_lookup = lookup_serve.shape[1] // devices
    block = -(-cap_lookup // 8) * 8
    enc_width = time_freq.shape[0]
    edge_width = edge_features.shape[1]
    freq, phase = time_freq[None, :], time_phase[None, :]
    shape, sent_shape = jax.ShapeDtypeStruct, pltpu.HBM

    shared = cores_share(gru_weight)
    total, half = gru_weight.shape[0], gru_weight.shape[1] // 2
    (rows,) = call(
        serve_kernel,
        "serve_endpoints",
        (sent_shape((slots, width), BF),),
        (),
        (update_serve, memory),
        (),
        fetched=(update_serve, memory),
        scratch=(pltpu.VMEM((slots, width), BF),),
        left=(0,),
        extra_sems=2,
    )
    if shared:
        late_weight = after(gru_weight, rows)
        side, column_at = rest_index // 2 % 2, rest_index % 2 * half
        first = other_ev(
            lax.dynamic_slice(late_weight, (side * SHARED, column_at), (SHARED, half))
        )
        piece = half
        core, other = rest_index % 2, 2 * (1 - ev)
        place = [2 * ev, 2 * ev + 1, other + core, other + 1 - core]
    else:
        whole = lax.all_gather(gru_weight, "ev", axis=1, tiled=True)
        piece, place = whole.shape[1], [jnp.int32(0)]
    scalars = jnp.stack([hi] + place + [rest_index // 2 % 2]).astype(jnp.int32)
    fetched = exchange(rows.reshape(devices, cap, width), BOTH).reshape(slots, width)

    lookup_row = lookup_serve
    if block != cap_lookup:
        lookup_row = jnp.pad(
            lookup_serve.reshape(devices, cap_lookup),
            ((0, 0), (0, block - cap_lookup)),
            constant_values=-1,
        ).reshape(1, devices * block)
    raw = (
        after(update_serve, rows),
        last_time[None, :],
        event_time[None, :],
        edge_features.T,
        update_slot.T,
        lookup_row,
        freq,
        phase,
    )
    rows_shape = pltpu.VMEM((near * block // LANES, LANES), F32)
    packed = cap % 16 == 0
    sent_lines = (devices, cap // 2, LANES) if packed else (slots, LANES)
    message_shape = (slots, width + LANES)
    if packed:
        message_shape = (devices, cap * width // LANES + cap // 2, LANES)
    tau, swap, sent, near_index, away_index = call(
        functools.partial(prepare_kernel, enc_width, sizes),
        "prepare",
        (
            pltpu.VMEM((slots + 16, LANES), F32),
            pltpu.VMEM((slots, slots), BF),
            pltpu.VMEM(sent_lines, BF),
            rows_shape,
            rows_shape,
        ),
        (scalars,),
        raw,
        (),
        fetched=raw,
        scratch=(pltpu.VMEM((devices * block, LANES), F32),),
    )
    if shared:
        sent = after(sent, first)
    message = call(
        partner_kernel,
        "partner_rows",
        sent_shape(message_shape, BF),
        (),
        (),
        (fetched,),
        kept=(swap, sent),
    )
    if shared:
        late_weight = after(gru_weight, rows)
        lower = other_ev(lax.dynamic_slice(late_weight, (DIRECT, column_at), (total - DIRECT, half)))
        first = after(first, message)
        second = other_x(first)
        pieces = [first, second, after(lower, second)]
        pieces += [other_core(x) for x in pieces]
    else:
        pieces = [whole]
    message = exchange(message.reshape(devices, -1, message_shape[-1]), BOTH)
    raw = (update_serve, memory, gru_bias, gru_weight)
    parts = pltpu.VMEM((3 * width // piece, nodes, piece), F32)
    new_memory, extended, near_rows = call(
        functools.partial(update_kernel, enc_width, edge_width, shared),
        "update_memory",
        (
            sent_shape((nodes, width), BF),
            sent_shape((nodes + 16, width), BF),
            sent_shape((near * block, width), BF),
        ),
        (scalars, hub_node),
        raw,
        (message.reshape(message_shape), *pieces),
        kept=(tau, near_index, away_index),
        fetched=raw,
        scratch=(
            parts,
            parts,
            pltpu.VMEM((nodes + 16, width), BF),
            pltpu.VMEM((near * block, width), BF),
        ),
        left=(0, 1, 2),
        limit=28,
    )
    other_extended = other_half(extended)
    near_looked = exchange(near_rows.reshape(near, block, width), NEAR)
    far_rows = call(
        far_kernel,
        "far_rows",
        sent_shape((near, block * width // LANES + 8, LANES), BF),
        (),
        (extended,),
        (other_extended,),
        fetched=(shape((16, width), BF),),
        flops=3 * 10**10,
    )
    far_looked = exchange(far_rows, NEAR)
    raw = (lookup_slot.T, hub_choice.T, neighbour_gap.T, freq, phase)
    routes, near_count = lookup_slot.shape[1] * events, neighbour_gap.shape[1] * events
    picked, pick_far, pick_hub, enc, own_enc = call(
        functools.partial(pick_kernel, cap_lookup, sizes[1:]),
        "pick_near",
        (
            pltpu.VMEM((routes, width), BF),
            pltpu.VMEM(lookup_slot.T.shape, F32),
            pltpu.VMEM(hub_choice.T.shape, F32),
            sent_shape((near_count, LANES), BF),
            pltpu.VMEM((8, LANES), BF),
        ),
        (scalars,),
        raw,
        (near_looked,),
        fetched=raw,
    )
    raw = (keyval_weight, enc, query_weight, output_weight)
    embedding = call(
        attend_kernel,
        "attend",
        sent_shape((events, width), BF),
        (),
        raw,
        (far_looked,),
        kept=(picked, pick_far, pick_hub, own_enc),
        fetched=raw,
    )
    return (new_memory, embedding)


def solution(mesh):
    ev_size, mem_size = mesh.devices.shape
    split = jax.sharding.Mesh(mesh.devices.reshape(ev_size, 2, 2, mem_size // 4), BOTH)
    both = P(BOTH)
    rows = P(BOTH, None)
    return jax.shard_map(
        local,
        mesh=split,
        in_specs=(
            rows,
            both,
            both,
            rows,
            rows,
            rows,
            rows,
            rows,
            rows,
            both,
            rows,
            P(),
            P(),
            P(None, "ev"),
            P(),
            P(),
            P(),
            P(),
        ),
        out_specs=(rows, rows),
        check_vma=False,
    )
```
